256 devices in a mesh: tx: 16 (over x_lo, y, core), ty: 16 (over x_hi, z).
Axes of the slice: x: 4 (x_hi: 2, x_lo: 2; x = x_hi * 2 + x_lo), y: 4, z: 8, core: 2. Of those that a mesh axis runs over, the one named last changes fastest.
Arguments:
- velocity: float32 [3, 48, 128, 2048], P(None, None, 'tx', 'ty'), may hold values from -6 to 6
- pressure: float32 [48, 128, 2048], P(None, 'tx', 'ty'), may hold values from -6 to 6
- drag_rate: float32 [48, 128, 2048], P(None, 'tx', 'ty'), may hold values from 0.5 to 4
- forcing: float32 [2, 48, 128, 2048], P(None, None, 'tx', 'ty'), may hold values from -6 to 6
- site_velocity: float32 [3, 16, 8, 32768], P(None, None, None, ('tx', 'ty')), may hold values from -6 to 6
- site_pressure: float32 [16, 8, 32768], P(None, None, ('tx', 'ty')), may hold values from -6 to 6
- site_drag: float32 [16, 8, 32768], P(None, None, ('tx', 'ty')), may hold values from 0.5 to 4
- site_forcing: float32 [2, 16, 8, 32768], P(None, None, None, ('tx', 'ty')), may hold values from -6 to 6
- owners: int32 [256], replicated, may hold values from 0 to 9, as said below
- sweep_counts: int32 [10], replicated, may hold values from 3 to 6
- parent_cells: int32 [4096, 1024], P(('tx', 'ty')), may hold values from 0 to 49151
- point_slots: int32 [2, 1114112], P(None, ('tx', 'ty')), may hold values from 0 to 16383
- point_weights: int32 [1114112], P(('tx', 'ty')), may hold values from 0 to 3
Outputs:
- new_velocity: float32 [3, 48, 128, 2048], P(None, None, 'tx', 'ty')
- new_pressure: float32 [48, 128, 2048], P(None, 'tx', 'ty')
- new_site_velocity: float32 [3, 16, 8, 32768], P(None, None, None, ('tx', 'ty'))
- new_site_pressure: float32 [16, 8, 32768], P(None, None, ('tx', 'ty'))
The draws below stay inside these ranges and needn't reach their ends.
Inputs may be any that keep to these rules, and one draw needn't show every extreme that they name: `owners`: never falls from one device to the next; each of the 10 sites owns one device or more, so its blocks are consecutive. `parent_cells`: row d * 16 + p names a cell of the regional tile at device d's tx index and ty index p, flattened over (height, x, y) within the tile. `point_slots`: the flattened pair p * 1024 + s of the same device's requests. `point_weights`: numerator k of the first parent's weight (2 k + 1) / 8.
All inputs are finite; a program needn't handle non-finite values.
Results may differ from the reference program's by a relative error of at most 0.00002.
Values sent between devices are 32-bit elements; how exact they have to be, the bound alone decides.
A program may use at most 128 MiB of HBM per device.

```python
import math
import jax
import jax.numpy as jnp

NZ = 48
CX = 8
CY = 128
SZ = 16
SX = 8
SLAB = 128
CAP = 1024
SWEEPS = 8
SSWEEPS = 6
NSITE = 10
NDEV = 256
ROW_DEVICES = 16
NX = 128
NY = 2048
SY = 32768
BPTS = 4352


def draw_owners(key, part):
    key = jax.random.fold_in(key, 11)
    cuts = jax.random.permutation(key, NDEV - 1)[:NSITE - 1] + 1
    places = jnp.arange(NDEV, dtype=jnp.int32)
    return jnp.sum((cuts[None, :] <= places[:, None]).astype(jnp.int32), axis=1).astype(jnp.int32)


def draw_sweep_counts(key, part):
    key = jax.random.fold_in(key, 23)
    count_key, order_key = jax.random.split(key)
    counts = jax.random.randint(count_key, (NSITE,), SSWEEPS // 2, SSWEEPS + 1).astype(jnp.int32)
    order = jax.random.permutation(order_key, NSITE)
    counts = counts.at[order[0]].set(SSWEEPS)
    counts = counts.at[order[1]].set(SSWEEPS // 2)
    return counts.astype(jnp.int32)


def place_ends(drawn, rng, smallest, largest):
    spot = [jax.random.randint(jax.random.fold_in(rng, axis), (), 0, length) for axis, length in enumerate(drawn.shape)]
    longest = drawn.shape.index(max(drawn.shape))
    beside = spot[:longest] + [(spot[longest] + 1) % drawn.shape[longest]] + spot[longest + 1:]
    return drawn.at[tuple(spot)].set(smallest).at[tuple(beside)].set(largest)


def levels(stream_key, shape, cuts, smallest, high):
    level, own = 1.0, jax.random.fold_in(stream_key, 6)
    for position, parts in cuts:
        heights = jnp.exp(jax.random.uniform(jax.random.fold_in(own, position), (parts,), jnp.float32, smallest / len(cuts), high / len(cuts)))
        level = level * jnp.repeat(heights, shape[position] // parts).reshape([-1 if axis == position else 1 for axis in range(len(shape))])
    return level


def noise(rng, dims, width, bound, shards=(), kind=jnp.bfloat16):
    gain = levels(rng, dims, shards, -0.22, 0.18) if shards else 1.0
    array = jax.random.normal(rng, dims, jnp.float32) * width * gain
    return jnp.minimum(jnp.maximum(array, -bound), bound).astype(kind)


def setup_inputs(seed: int = 0) -> dict:
    key_list = jax.random.split(jax.random.key(seed), 14)
    return {
        "velocity": noise(key_list[0], (3, NZ, NX, NY), 1.0, 6.0, ((2, 16), (3, 16)), jnp.float32),
        "pressure": noise(key_list[1], (NZ, NX, NY), 1.0, 6.0, ((1, 16), (2, 16)), jnp.float32),
        "drag_rate": jnp.clip(jnp.exp(math.log(4.0) - 2.0794415 * jax.random.uniform(key_list[2], (NZ, NX, NY), jnp.float32) ** levels(key_list[2], (NZ, NX, NY), ((1, 16), (2, 16)), -0.2, 0.2)), 0.5, 4.0),
        "forcing": noise(key_list[3], (2, NZ, NX, NY), 1.0, 6.0, ((2, 16), (3, 16)), jnp.float32),
        "site_velocity": noise(key_list[4], (3, SZ, SX, SY), 1.0, 6.0, ((3, 256),), jnp.float32),
        "site_pressure": noise(key_list[5], (SZ, SX, SY), 1.0, 6.0, ((2, 256),), jnp.float32),
        "site_drag": jnp.clip(jnp.exp(math.log(4.0) - 2.0794415 * jax.random.uniform(key_list[6], (SZ, SX, SY), jnp.float32) ** levels(key_list[6], (SZ, SX, SY), ((2, 256),), -0.2, 0.2)), 0.5, 4.0),
        "site_forcing": noise(key_list[7], (2, SZ, SX, SY), 1.0, 6.0, ((3, 256),), jnp.float32),
        "owners": draw_owners(jax.random.fold_in(key_list[13], 71), 0),
        "sweep_counts": draw_sweep_counts(jax.random.fold_in(key_list[13], 71), 0),
        "parent_cells": place_ends(jax.random.randint(key_list[10], (NDEV * ROW_DEVICES, CAP), 0, NZ * CX * CY), jax.random.fold_in(key_list[10], 1), 0, (NZ * CX * CY) - 1).astype(jnp.int32),
        "point_slots": place_ends(jax.random.randint(key_list[11], (2, NDEV * BPTS), 0, ROW_DEVICES * CAP), jax.random.fold_in(key_list[11], 1), 0, (ROW_DEVICES * CAP) - 1).astype(jnp.int32),
        "point_weights": place_ends(jax.random.randint(key_list[12], (NDEV * BPTS,), 0, 4), jax.random.fold_in(key_list[12], 1), 0, 3).astype(jnp.int32),
    }


viscosity = 1.0
relax_factor = 0.3


def vertical_pair(values):
    zero_layer = jnp.zeros_like(values[..., :1, :, :])
    lower_cell = jnp.concatenate([zero_layer, values[..., :-1, :, :]], axis=-3)
    upper_cell = jnp.concatenate([values[..., 1:, :, :], zero_layer], axis=-3)
    return lower_cell, upper_cell


def neighbour_sum(values, neighbours):
    lower_cell, upper_cell = vertical_pair(values)
    return neighbours[0] + neighbours[1] + neighbours[2] + neighbours[3] + lower_cell + upper_cell


def gradient(values, neighbours):
    lower_cell, upper_cell = vertical_pair(values)
    return jnp.concatenate([(neighbours[1] - neighbours[0]) * 0.5, (neighbours[3] - neighbours[2]) * 0.5, (upper_cell - lower_cell) * 0.5], axis=0)


def divergence(predicted, neighbours):
    lower_cell, upper_cell = vertical_pair(predicted[2:3])
    return ((neighbours[1][0] - neighbours[0][0]) + (neighbours[3][1] - neighbours[2][1]) + (upper_cell[0] - lower_cell[0])) * 0.5


def predictor(fields, neighbours, drag_rate, forcing):
    velocity_sum = neighbour_sum(fields[:3], [member[:3] for member in neighbours])
    pressure_push = gradient(fields[3:], [member[3:] for member in neighbours])
    source = jnp.concatenate([forcing, jnp.zeros_like(forcing[:1])], axis=0)
    diagonal = 6.0 * viscosity + drag_rate
    return (viscosity * velocity_sum + source - pressure_push) / diagonal, diagonal


def padded_sides(padded):
    return [padded[..., :-2, 1:-1], padded[..., 2:, 1:-1], padded[..., 1:-1, :-2], padded[..., 1:-1, 2:]]


def pad_plane(values):
    widths = [(0, 0)] * (values.ndim - 2) + [(1, 1), (1, 1)]
    return jnp.pad(values, widths)


def regional_step(velocity, pressure, drag_rate, forcing):
    fields = jnp.concatenate([velocity, pressure[None]], axis=0)
    predicted, diagonal = predictor(fields, padded_sides(pad_plane(fields)), drag_rate, forcing)
    source_term = divergence(predicted, padded_sides(pad_plane(predicted))) * diagonal
    correction = -source_term / 6.0
    for sweep_index in range(1, SWEEPS):
        stacked = correction[None]
        spread = neighbour_sum(stacked, padded_sides(pad_plane(stacked)))[0]
        correction = (spread - source_term) / 6.0
    stacked = correction[None]
    pressure_push = gradient(stacked, padded_sides(pad_plane(stacked)))
    return predicted - pressure_push / diagonal, pressure + relax_factor * correction


def plane_values(fields, parent_cells, point_slots, point_weights):
    requested = parent_cells.reshape(NDEV, ROW_DEVICES, CAP)
    tile_row = (jnp.arange(NDEV, dtype=jnp.int32) // ROW_DEVICES)[:, None, None]
    peer_index = jnp.arange(ROW_DEVICES, dtype=jnp.int32)[None, :, None]
    layer_index = requested // (CX * CY)
    within = requested % (CX * CY)
    column = tile_row * CX + within // CY
    across = peer_index * CY + within % CY
    flat_index = (layer_index * NX + column) * NY + across
    fetched = jnp.take(fields.reshape(4, -1), flat_index.reshape(-1), axis=1).reshape(4, NDEV, ROW_DEVICES * CAP)
    slot_pairs = point_slots.reshape(2, NDEV, BPTS)
    weight_first = (2.0 * point_weights.reshape(NDEV, BPTS).astype(jnp.float32) + 1.0) / 8.0
    first_value = jnp.take_along_axis(fetched, slot_pairs[0][None], axis=2)
    second_value = jnp.take_along_axis(fetched, slot_pairs[1][None], axis=2)
    return weight_first * first_value + (1.0 - weight_first) * second_value


def site_sides(values, west_plane, east_plane, south_plane, north_plane, site_starts, site_ends):
    west_side = jnp.concatenate([west_plane[:, :, None, :], values[:, :, :-1, :]], axis=2)
    east_side = jnp.concatenate([values[:, :, 1:, :], east_plane[:, :, None, :]], axis=2)
    blocked = values.reshape(values.shape[:3] + (NDEV, SLAB))
    empty_block = jnp.zeros_like(blocked[..., :1, :1])
    prior_column = jnp.concatenate([empty_block, blocked[..., :-1, -1:]], axis=3)[..., 0]
    next_column = jnp.concatenate([blocked[..., 1:, :1], empty_block], axis=3)[..., 0]
    prior_column = jnp.where(site_starts, south_plane, prior_column)
    next_column = jnp.where(site_ends, north_plane, next_column)
    south_side = jnp.concatenate([prior_column[..., None], blocked[..., :-1]], axis=4).reshape(values.shape)
    north_side = jnp.concatenate([blocked[..., 1:], next_column[..., None]], axis=4).reshape(values.shape)
    return [west_side, east_side, south_side, north_side]


def site_step(fields, drag_rate, forcing, planes, site_starts, site_ends, allowed):
    west_plane, east_plane, south_plane, north_plane = planes
    neighbours = site_sides(fields, west_plane, east_plane, south_plane, north_plane, site_starts, site_ends)
    predicted, diagonal = predictor(fields, neighbours, drag_rate, forcing)
    moved_sides = site_sides(predicted, west_plane[:3], east_plane[:3], south_plane[:3], north_plane[:3], site_starts, site_ends)
    source_term = divergence(predicted, moved_sides) * diagonal
    blank_x = jnp.zeros_like(west_plane[:1])
    blank_y = jnp.zeros_like(south_plane[:1])
    correction = -source_term / 6.0
    for sweep_index in range(1, SSWEEPS):
        stacked = correction[None]
        spread = neighbour_sum(stacked, site_sides(stacked, blank_x, blank_x, blank_y, blank_y, site_starts, site_ends))[0]
        correction = jnp.where(sweep_index < allowed, (spread - source_term) / 6.0, correction)
    stacked = correction[None]
    pressure_push = gradient(stacked, site_sides(stacked, blank_x, blank_x, blank_y, blank_y, site_starts, site_ends))
    return predicted - pressure_push / diagonal, fields[3] + relax_factor * correction


def reference(velocity, pressure, drag_rate, forcing, site_velocity, site_pressure, site_drag, site_forcing, owners, sweep_counts, parent_cells, point_slots, point_weights):
    new_velocity, new_pressure = regional_step(velocity, pressure, drag_rate, forcing)
    fields = jnp.concatenate([velocity, pressure[None]], axis=0)
    values = plane_values(fields, parent_cells, point_slots, point_weights)
    plane_size = SZ * SLAB
    end_size = SZ * SX
    west_plane = values[:, :, :plane_size].reshape(4, NDEV, SZ, SLAB).transpose(0, 2, 1, 3).reshape(4, SZ, NDEV * SLAB)
    east_plane = values[:, :, plane_size:2 * plane_size].reshape(4, NDEV, SZ, SLAB).transpose(0, 2, 1, 3).reshape(4, SZ, NDEV * SLAB)
    south_plane = values[:, :, 2 * plane_size:2 * plane_size + end_size].reshape(4, NDEV, SZ, SX).transpose(0, 2, 3, 1)
    north_plane = values[:, :, 2 * plane_size + end_size:].reshape(4, NDEV, SZ, SX).transpose(0, 2, 3, 1)
    places = jnp.arange(NDEV, dtype=jnp.int32)
    previous = owners[jnp.maximum(places - 1, 0)]
    following = owners[jnp.minimum(places + 1, NDEV - 1)]
    site_starts = (places == 0) | (owners != previous)
    site_ends = (places == NDEV - 1) | (owners != following)
    allowed = jnp.repeat(sweep_counts[owners], SLAB)
    site_fields = jnp.concatenate([site_velocity, site_pressure[None]], axis=0)
    new_site_velocity, new_site_pressure = site_step(site_fields, site_drag, site_forcing, (west_plane, east_plane, south_plane, north_plane), site_starts, site_ends, allowed)
    return new_velocity, new_pressure, new_site_velocity, new_site_pressure
```

```python
import functools

import jax
import jax.numpy as jnp
from jax import lax
from jax.experimental import pallas as pl
from jax.experimental.pallas import tpu as pltpu
from jax.sharding import PartitionSpec as P

F32 = jnp.float32
BF16 = jnp.bfloat16
MESH = pl.DeviceIdType.MESH

NZ = 48
SZ = 16
CAP = 1024
SWEEPS = 8
SSWEEPS = 6
RELAX = 0.3
SIXTH = 1.0 / 6.0
CHUNK = 512
POINTS = 4352
PCHUNK = 256


def one_hot(key, depth):
    n = key.shape[1]
    rows = lax.broadcasted_iota(jnp.int32, (256, n), 0).astype(BF16)
    parts = []
    for b in range(depth // 256):
        low = jnp.where((key >> 8) == b, key & 255, -1) if depth > 256 else key
        low = jnp.broadcast_to(low.astype(F32).astype(BF16), (256, n))
        parts.append(jnp.where(rows == low, jnp.ones((), BF16), jnp.zeros((), BF16)))
    return jnp.concatenate(parts, axis=0) if len(parts) > 1 else parts[0]


def pieces(v):
    hi = v.astype(BF16)
    return hi, (v - hi.astype(F32)).astype(BF16)


def kernel(
    row,
    rows_tx,
    vel,
    pre,
    drag,
    forc,
    svel,
    spre,
    sdrag,
    sforc,
    owners,
    counts,
    cells,
    slots,
    weights,
    nvel,
    npre,
    nsvel,
    nspre,
    sidx,
    ridx,
    table,
    rep,
    got,
    table2,
    planes,
    xs,
    xr,
    ys,
    yr,
    pred,
    pxs,
    pxr,
    pys,
    pyr,
    src,
    hs,
    hr,
    hm,
    hx,
    corr,
    sps,
    spr,
    sh,
    wes,
    wer,
    wem,
    idx_send,
    idx_recv,
    rep_send,
    rep_recv,
    halo_send,
    halo_recv,
):
    tx = lax.axis_index("tx")
    ty = lax.axis_index("ty")
    me = tx * row + ty
    total = row * rows_tx

    def device(a, b):
        return {"tx": a, "ty": b}

    def place(d):
        return device(d // row, lax.rem(d, row))

    x_before = device(lax.rem(tx + rows_tx - 1, rows_tx), ty)
    x_after = device(lax.rem(tx + 1, rows_tx), ty)
    y_before = device(tx, lax.rem(ty + row - 1, row))
    y_after = device(tx, lax.rem(ty + 1, row))
    d_before = place(lax.rem(me + total - 1, total))
    d_after = place(lax.rem(me + 1, total))

    barrier = pltpu.get_barrier_semaphore()
    for t in range(1, row):
        pl.semaphore_signal(
            barrier, inc=1, device_id=device(tx, lax.rem(ty + t, row)), device_id_type=MESH
        )
    for there in (x_before, x_after, d_before, d_after):
        pl.semaphore_signal(barrier, inc=1, device_id=there, device_id_type=MESH)

    lane = lax.broadcasted_iota(jnp.int32, (8, 128), 1)
    sub = lax.broadcasted_iota(jnp.int32, (8, 128), 0)
    zero = jnp.zeros((8, 128), F32)

    def up(v):
        return pltpu.roll(v, 1, v.ndim - 1)

    def down(v):
        return pltpu.roll(v, 127, v.ndim - 1)

    def sub_up(v):
        return pltpu.roll(v, 1, v.ndim - 2)

    def sub_down(v):
        return pltpu.roll(v, 7, v.ndim - 2)

    def copy(src_ref, dst_ref, number, there):
        return pltpu.make_async_remote_copy(
            src_ref=src_ref,
            dst_ref=dst_ref,
            send_sem=halo_send.at[number],
            recv_sem=halo_recv.at[number],
            device_id=there,
            device_id_type=MESH,
        )

    field = [vel.at[0], vel.at[1], vel.at[2], pre]

    for p in range(row):
        sidx[p] = cells[p : p + 1, :]

    for f in range(4):
        xs[0, f] = field[f][:, 0, :]
        xs[1, f] = field[f][:, 7, :]

    def pack_fields(zz, acc):
        acc = list(acc)
        for f in range(4):
            j = f * 16 + zz
            here = (lane >> 1) == j
            for g in range(3):
                acc[g] = jnp.where(
                    here, pltpu.roll(field[f][g * 16 + zz], 2 * j + 1, 1), acc[g]
                )
        return tuple(acc)

    acc = lax.fori_loop(0, 16, pack_fields, (zero,) * 3)
    for g in range(3):
        ys[g] = acc[g]

    sfield = [svel.at[0], svel.at[1], svel.at[2], spre, sdrag, sforc.at[0], sforc.at[1]]

    def pack_site(j, acc):
        acc = list(acc)
        here = (lane >> 4) == j
        for f in range(7):
            for g in range(2):
                acc[2 * f + g] = jnp.where(
                    here, pltpu.roll(sfield[f][g * 8 + j], 16 * j + 8, 1), acc[2 * f + g]
                )
        return tuple(acc)

    acc = lax.fori_loop(0, 8, pack_site, (zero,) * 14)
    for g in range(14):
        sps[g] = acc[g]

    pl.semaphore_wait(barrier, row - 1 + 4)

    def index_copy(to, slot):
        return pltpu.make_async_remote_copy(
            src_ref=sidx.at[to],
            dst_ref=ridx.at[ty],
            send_sem=idx_send.at[to],
            recv_sem=idx_recv.at[slot],
            device_id=device(tx, to),
            device_id_type=MESH,
        )

    for t in range(1, row):
        index_copy(lax.rem(ty + t, row), ty).start()

    fields_x = [copy(xs.at[0], xr.at[1], 0, x_before), copy(xs.at[1], xr.at[0], 1, x_after)]
    fields_y = [copy(ys, yr.at[1], 2, y_before), copy(ys, yr.at[0], 3, y_after)]
    site_y = [copy(sps, spr.at[1], 4, d_before), copy(sps, spr.at[0], 5, d_after)]
    pred_x = [copy(pxs.at[0], pxr.at[1], 6, x_before), copy(pxs.at[1], pxr.at[0], 7, x_after)]
    pred_y = [copy(pys, pyr.at[1], 8, y_before), copy(pys, pyr.at[0], 9, y_after)]
    src_y = [copy(hs, hr.at[1], 10, y_before), copy(hs, hr.at[0], 11, y_after)]
    src_x = [copy(src.at[1], src.at[2], 12, x_before), copy(src.at[1], src.at[0], 13, x_after)]
    corner_x = [copy(hm.at[1], hm.at[2], 14, x_before), copy(hm.at[1], hm.at[0], 15, x_after)]
    plane_y = [copy(wes, wer.at[1], 16, d_before), copy(wes, wer.at[0], 17, d_after)]

    def start(pair):
        for c in pair:
            c.start()

    def arrive(pair):
        for c in pair:
            c.wait_recv()

    start(fields_x)
    start(fields_y)
    start(site_y)

    for f in range(4):
        for x in range(8):
            hi, lo = pieces(field[f][:, x, :])
            table[f * NZ : (f + 1) * NZ, x * 128 : (x + 1) * 128] = hi
            table[(4 + f) * NZ : (5 + f) * NZ, x * 128 : (x + 1) * 128] = lo

    def lookup(q):
        for c in range(CAP // CHUNK):
            v = ridx[q, :, c * CHUNK : (c + 1) * CHUNK]
            found = jnp.dot(table[...], one_hot(v & 1023, 1024), preferred_element_type=F32)
            layer = lax.broadcasted_iota(jnp.int32, (NZ, CHUNK), 0) == (v >> 10)
            for f in range(4):
                s = found[f * NZ : (f + 1) * NZ] + found[(4 + f) * NZ : (5 + f) * NZ]
                s = jnp.sum(jnp.where(layer, s, 0.0), axis=0, keepdims=True)
                for k in range(CHUNK // 128):
                    r = c * (CHUNK // 128) + k
                    rep[q, f, r : r + 1, :] = s[:, k * 128 : (k + 1) * 128]

    def reply_copy(to, slot):
        return pltpu.make_async_remote_copy(
            src_ref=rep.at[to],
            dst_ref=got.at[ty],
            send_sem=rep_send.at[to],
            recv_sem=rep_recv.at[slot],
            device_id=device(tx, to),
            device_id_type=MESH,
        )

    def serve(t, _):
        q = lax.rem(ty + row - t, row)
        index_copy(q, q).wait_recv()
        lookup(q)
        reply_copy(q, ty).start()
        return 0

    ridx[ty] = sidx[ty]
    lookup(ty)
    got[ty] = rep[ty]

    has_x = [jnp.where(tx > 0, 1.0, 0.0), jnp.where(tx < rows_tx - 1, 1.0, 0.0)]
    has_y = [jnp.where(ty > 0, 1.0, 0.0), jnp.where(ty < row - 1, 1.0, 0.0)]
    edge_y = jnp.where(lane < 64, has_y[0], has_y[1])

    arrive(fields_x)
    arrive(fields_y)
    for g in range(3):
        first = (lane & 1) == 0
        yr[0, g] = jnp.where(first, down(yr[1, g]), up(yr[0, g]))

    def below(ref, z):
        v = ref[jnp.maximum(z - 1, 0)]
        return v * jnp.where(z > 0, 1.0, 0.0)

    def above(ref, z):
        v = ref[jnp.minimum(z + 1, NZ - 1)]
        return v * jnp.where(z < NZ - 1, 1.0, 0.0)

    def x_sides(v, low, high):
        low = jnp.broadcast_to(low, (8, 128)) * has_x[0]
        high = jnp.broadcast_to(high, (8, 128)) * has_x[1]
        return jnp.where(sub == 0, low, sub_up(v)), jnp.where(sub == 7, high, sub_down(v))

    def y_sides(v, edge):
        edge = edge * edge_y
        return jnp.where(lane == 0, edge, up(v)), jnp.where(lane == 127, edge, down(v))

    def predict(zz, packed):
        for g in range(3):
            z = g * 16 + zz
            inverse = 1.0 / (6.0 + drag[z])
            sides = []
            for f in range(4):
                v = field[f][z]
                xm, xp = x_sides(v, xr[0, f, pl.ds(z, 1), :], xr[1, f, pl.ds(z, 1), :])
                k = 2 * (f * 16 + zz) + 1
                ym, yp = y_sides(v, pltpu.roll(yr[0, g], 128 - k, 1))
                sides.append((xm, xp, ym, yp, below(field[f], z), above(field[f], z)))
            push = sides[3]
            push = [(push[1] - push[0]) * 0.5, (push[3] - push[2]) * 0.5, (push[5] - push[4]) * 0.5]
            out = []
            for i in range(3):
                s = sides[i]
                n = ((s[0] + s[1]) + (s[2] + s[3])) + (s[4] + s[5])
                if i < 2:
                    n = n + forc[i, z]
                out.append((n - push[i]) * inverse)
                pred[i, z] = out[i]
            packed = jnp.where((lane >> 1) == z, pltpu.roll(out[1], 2 * z + 1, 1), packed)
        return packed

    pys[...] = lax.fori_loop(0, 16, predict, zero)
    pxs[0] = pred[0, :, 0, :]
    pxs[1] = pred[0, :, 7, :]
    start(pred_x)
    start(pred_y)

    lax.fori_loop(1, 4, serve, 0)

    arrive(pred_x)
    arrive(pred_y)
    first = (lane & 1) == 0
    edges_v = jnp.where(first, down(pyr[1]), up(pyr[0]))

    def source(j, packed):
        packed = list(packed)
        for g in range(6):
            z = g * 8 + j
            xm, xp = x_sides(pred[0, z], pxr[0, pl.ds(z, 1), :], pxr[1, pl.ds(z, 1), :])
            ym, yp = y_sides(pred[1, z], pltpu.roll(edges_v, 127 - 2 * z, 1))
            div = (xp - xm) + (yp - ym) + (above(pred.at[2], z) - below(pred.at[2], z))
            s = div * 0.5 * (6.0 + drag[z])
            src[1, z] = s
            packed[g] = jnp.where((lane >> 4) == j, pltpu.roll(s, 16 * j + 8, 1), packed[g])
        return tuple(packed)

    acc = lax.fori_loop(0, 8, source, (zero,) * 6)
    for g in range(6):
        hs[g] = acc[g]
    start(src_y)

    lax.fori_loop(4, 7, serve, 0)

    arrive(src_y)
    left = ((lane >> 3) & 1) == 0
    for g in range(6):
        hm[1, g] = jnp.where(left, hr[0, g], hr[1, g])
    start(src_x)
    start(corner_x)

    lax.fori_loop(7, row, serve, 0)

    arrive(src_x)
    arrive(corner_x)
    inside = []
    for b in range(3):
        m = (has_x[0], 1.0, has_x[1])[b] * SIXTH
        inside.append((jnp.full((8, 128), m, F32), edge_flip(lane, has_y) * m))

    for b in range(3):
        for h in range(2):
            for n in range(2):
                corr[n, b, h, 0] = zero
                corr[n, b, h, NZ + 1] = zero

    def widen(j, _):
        for b in range(3):
            for g in range(6):
                z = g * 8 + j
                s = pltpu.roll(hm[b, g], 120 - 16 * j, 1)
                hx[b, z] = s
                corr[0, b, 1, z + 1] = -s * inside[b][1]
                corr[0, b, 0, z + 1] = -src[b, z] * inside[b][0]
        return 0

    lax.fori_loop(0, 8, widen, 0)

    def neighbours(now, z):
        out = {}
        c = {(b, h): corr[now, b, h, z + 1] for b in range(3) for h in range(2)}
        for h in range(2):
            lift = [sub_up(c[b, h]) for b in range(3)]
            drop = [sub_down(c[b, h]) for b in range(3)]
            for b in range(3):
                xm = jnp.where(sub == 0, lift[max(b - 1, 0)], lift[b])
                xp = jnp.where(sub == 7, drop[min(b + 1, 2)], drop[b])
                out[b, h] = [xm, xp]
        for b in range(3):
            u = [up(c[b, h]) for h in range(2)]
            d = [down(c[b, h]) for h in range(2)]
            for h in range(2):
                ym = jnp.where(lane == 0, u[1 - h], u[h])
                yp = jnp.where(lane == 127, d[1 - h], d[h])
                out[b, h] += [ym, yp]
        return out

    ZB = 4

    def sweep(k, _):
        now = lax.rem(k, 2)
        later = 1 - now

        def layers(i, _):
            for zi in range(ZB):
                z = i * ZB + zi
                sides = neighbours(now, z)
                for b in range(3):
                    for h in range(2):
                        s = sides[b, h]
                        n = ((s[0] + s[1]) + (s[2] + s[3])) + (
                            corr[now, b, h, z] + corr[now, b, h, z + 2]
                        )
                        t = src[b, z] if h == 0 else hx[b, z]
                        corr[later, b, h, z + 1] = (n - t) * inside[b][h]
            return 0

        lax.fori_loop(0, NZ // ZB, layers, 0)
        return 0

    lax.fori_loop(0, SWEEPS - 1, sweep, 0)
    last = (SWEEPS - 1) % 2

    def finish(z, _):
        c = [corr[last, b, 0, z + 1] for b in range(3)]
        e = corr[last, 1, 1, z + 1]
        xm = jnp.where(sub == 0, sub_up(c[0]), sub_up(c[1]))
        xp = jnp.where(sub == 7, sub_down(c[2]), sub_down(c[1]))
        ym = jnp.where(lane == 0, up(e), up(c[1]))
        yp = jnp.where(lane == 127, down(e), down(c[1]))
        half = 0.5 / (6.0 + drag[z])
        nvel[0, z] = pred[0, z] - (xp - xm) * half
        nvel[1, z] = pred[1, z] - (yp - ym) * half
        nvel[2, z] = pred[2, z] - (corr[last, 1, 0, z + 2] - corr[last, 1, 0, z]) * half
        npre[z] = pre[z] + RELAX * c[1]
        return 0

    lax.fori_loop(0, NZ, finish, 0)

    for t in range(1, row):
        q = lax.rem(ty + row - t, row)
        reply_copy(q, q).wait_recv()
    for f in range(4):
        for b in range(2):
            for u in range(row // 4):
                v = jnp.concatenate([got[4 * u + b, f], got[4 * u + 2 + b, f]], axis=0)
                hi, lo = pieces(v)
                r = f * 4 * row + u * 16
                table2[r : r + 16, b * 128 : (b + 1) * 128] = hi
                table2[16 * row + r : 16 * row + r + 16, b * 128 : (b + 1) * 128] = lo

    def point(c, _):
        at = pl.ds(pl.multiple_of(c * PCHUNK, PCHUNK), PCHUNK)
        j = jnp.concatenate([slots[0:1, at], slots[1:2, at]], axis=1)
        key = (j & 127) | (((j >> 10) & 1) << 7)
        m = ((j >> 11) << 3) | ((j >> 7) & 7)
        found = jnp.dot(table2[...], one_hot(key, 256), preferred_element_type=F32)
        here = lax.broadcasted_iota(jnp.int32, (4 * row, 2 * PCHUNK), 0) == m
        w = (2.0 * weights[:, at].astype(F32) + 1.0) * 0.125
        for f in range(4):
            r = f * 4 * row
            s = found[r : r + 4 * row] + found[16 * row + r : 16 * row + r + 4 * row]
            s = jnp.sum(jnp.where(here, s, 0.0), axis=0, keepdims=True)
            v = w * s[:, :PCHUNK] + (1.0 - w) * s[:, PCHUNK:]
            planes[f, pl.ds(2 * c, 1), :] = v[:, :128]
            planes[f, pl.ds(2 * c + 1, 1), :] = v[:, 128:]
        return 0

    lax.fori_loop(0, POINTS // PCHUNK, point, 0)

    acc = [zero, zero]
    for n in range(16):
        v = planes[n // 4, (n % 4) * 8 : (n % 4) * 8 + 8, :]
        j = n % 8
        acc[n // 8] = jnp.where((lane >> 4) == j, pltpu.roll(v, 16 * j + 8, 1), acc[n // 8])
    wes[0] = acc[0]
    wes[1] = acc[1]
    start(plane_y)

    own = owners[me]
    begins = (me == 0) | (owners[jnp.maximum(me - 1, 0)] != own)
    ends = (me == total - 1) | (owners[jnp.minimum(me + 1, total - 1)] != own)
    begins = jnp.full((8, 128), begins.astype(F32), F32)
    ends = jnp.full((8, 128), ends.astype(F32), F32)
    allowed = jnp.full((8, 128), counts[own], jnp.int32)
    other = jnp.where(lane < 64, ends, begins) > 0.5

    def ends_of(f):
        s = jnp.where((lane & 7) == sub, jnp.broadcast_to(planes[f, 32:33, :], (8, 128)), 0.0)
        n = jnp.where((lane & 7) == sub, jnp.broadcast_to(planes[f, 33:34, :], (8, 128)), 0.0)
        for k in (1, 2, 4):
            s = s + pltpu.roll(s, k, 1)
            n = n + pltpu.roll(n, 128 - k, 1)
        both = jnp.where((lane & 7) == 7, s, pltpu.roll(n, 8, 1))
        return [pltpu.roll(both, (120 - 8 * z) % 128, 1) for z in range(SZ)]

    outer = [jnp.stack(ends_of(f)) for f in range(4)]
    edge_lane = (lane == 0) | (lane == 127)

    def with_ends(v, f):
        return jnp.where((edge_lane & other)[None], outer[f], v)

    arrive(site_y)
    arrive(plane_y)
    left = ((lane >> 3) & 1) == 0
    for g in range(14):
        spr[0, g] = jnp.where(left, spr[0, g], spr[1, g])
    for n in range(7 * SZ):
        sh[n // SZ, n % SZ] = pltpu.roll(spr[0, n // 8], (120 - 16 * (n % 8)) % 128, 1)
    for g in range(2):
        v = jnp.where(left, wer[0, g], wer[1, g])
        for j in range(8):
            n = g * 8 + j
            wem[n // 4, (n % 4) * 8 : (n % 4) * 8 + 8, :] = pltpu.roll(v, (120 - 16 * j) % 128, 1)

    west = [[planes[f, 0:SZ, :], wem[f, 0:SZ, :]] for f in range(4)]
    east = [[planes[f, SZ : 2 * SZ, :], wem[f, SZ : 2 * SZ, :]] for f in range(4)]

    def layer_sides(v):
        blank = jnp.zeros((1, 8, 128), F32)
        return jnp.concatenate([blank, v[:-1]], axis=0), jnp.concatenate([v[1:], blank], axis=0)

    def site_x(v, h, f):
        shape = (SZ, 8, 128)
        if f is None:
            low = high = jnp.zeros(shape, F32)
        else:
            low = jnp.broadcast_to(west[f][h][:, None, :], shape)
            high = jnp.broadcast_to(east[f][h][:, None, :], shape)
        return jnp.where(sub[None] == 0, low, sub_up(v)), jnp.where(sub[None] == 7, high, sub_down(v))

    def site_y_sides(pair):
        u = [up(v) for v in pair]
        d = [down(v) for v in pair]
        return [
            (
                jnp.where(lane[None] == 0, u[1 - h], u[h]),
                jnp.where(lane[None] == 127, d[1 - h], d[h]),
            )
            for h in range(2)
        ]

    fields = [[sfield[f][...], with_ends(sh[f], f)] for f in range(4)]
    diag = [6.0 + sdrag[...], 6.0 + sh[4]]
    inverse = [1.0 / v for v in diag]
    force = [[sforc[i], sh[5 + i]] for i in range(2)]
    xside = [[site_x(fields[f][h], h, f) for h in range(2)] for f in range(4)]
    yside = [site_y_sides(fields[f]) for f in range(4)]
    moved = [[None, None] for _ in range(3)]
    for h in range(2):
        below_p, above_p = layer_sides(fields[3][h])
        push = [
            (xside[3][h][1] - xside[3][h][0]) * 0.5,
            (yside[3][h][1] - yside[3][h][0]) * 0.5,
            (above_p - below_p) * 0.5,
        ]
        for i in range(3):
            lo, hi = layer_sides(fields[i][h])
            n = (xside[i][h][0] + xside[i][h][1]) + (yside[i][h][0] + yside[i][h][1]) + (lo + hi)
            if i < 2:
                n = n + force[i][h]
            v = (n - push[i]) * inverse[h]
            moved[i][h] = with_ends(v, i) if h == 1 else v

    ys_v = site_y_sides(moved[1])
    term = []
    for h in range(2):
        xm, xp = site_x(moved[0][h], h, 0)
        lo, hi = layer_sides(moved[2][h])
        term.append(((xp - xm) + (ys_v[h][1] - ys_v[h][0]) + (hi - lo)) * 0.5 * diag[h])

    keep = [
        jnp.full((1, 8, 128), SIXTH, F32),
        jnp.where(other, 0.0, SIXTH)[None],
    ]
    e = [-term[h] * keep[h] for h in range(2)]
    for k in range(1, SSWEEPS):
        sides = site_y_sides(e)
        fresh = []
        for h in range(2):
            xm, xp = site_x(e[h], h, None)
            lo, hi = layer_sides(e[h])
            n = (xm + xp) + (sides[h][0] + sides[h][1]) + (lo + hi)
            fresh.append(jnp.where((allowed > k)[None], (n - term[h]) * keep[h], e[h]))
        e = fresh
    xm, xp = site_x(e[0], 0, None)
    ym, yp = site_y_sides(e)[0]
    lo, hi = layer_sides(e[0])
    half = 0.5 * inverse[0]
    nsvel[0] = moved[0][0] - (xp - xm) * half
    nsvel[1] = moved[1][0] - (yp - ym) * half
    nsvel[2] = moved[2][0] - (hi - lo) * half
    nspre[...] = spre[...] + RELAX * e[0]

    for pair in (fields_x, fields_y, site_y, pred_x, pred_y, src_y, src_x, corner_x, plane_y):
        for c in pair:
            c.wait_send()
    for t in range(1, row):
        q = lax.rem(ty + t, row)
        index_copy(q, q).wait_send()
        reply_copy(q, q).wait_send()


def edge_flip(lane, has_y):
    return jnp.where(lane < 64, has_y[1], has_y[0])


def shards(
    velocity,
    pressure,
    drag_rate,
    forcing,
    site_velocity,
    site_pressure,
    site_drag,
    site_forcing,
    owners,
    sweep_counts,
    parent_cells,
    point_slots,
    point_weights,
):
    row = lax.axis_size("ty")
    rows_tx = lax.axis_size("tx")
    vm = pl.BlockSpec(memory_space=pltpu.VMEM)
    sm = pl.BlockSpec(memory_space=pltpu.SMEM)

    def v(*shape):
        return pltpu.VMEM(shape, F32)

    out_shape = [
        jax.ShapeDtypeStruct(a.shape, F32)
        for a in (velocity, pressure, site_velocity, site_pressure)
    ]
    return pl.pallas_call(
        functools.partial(kernel, row, rows_tx),
        out_shape=out_shape,
        in_specs=[vm] * 8 + [sm] * 2 + [vm] * 3,
        out_specs=[vm] * 4,
        scratch_shapes=[
            pltpu.VMEM((row, 1, CAP), jnp.int32),
            pltpu.VMEM((row, 1, CAP), jnp.int32),
            pltpu.VMEM((8 * NZ, 1024), BF16),
            v(row, 4, 8, 128),
            v(row, 4, 8, 128),
            pltpu.VMEM((32 * row, 256), BF16),
            v(4, 40, 128),
            v(2, 4, NZ, 128),
            v(2, 4, NZ, 128),
            v(3, 8, 128),
            v(2, 3, 8, 128),
            v(3, NZ, 8, 128),
            v(2, NZ, 128),
            v(2, NZ, 128),
            v(8, 128),
            v(2, 8, 128),
            v(3, NZ, 8, 128),
            v(6, 8, 128),
            v(2, 6, 8, 128),
            v(3, 6, 8, 128),
            v(3, NZ, 8, 128),
            v(2, 3, 2, NZ + 2, 8, 128),
            v(14, 8, 128),
            v(2, 14, 8, 128),
            v(7, SZ, 8, 128),
            v(2, 8, 128),
            v(2, 2, 8, 128),
            v(4, 2 * SZ, 128),
            pltpu.SemaphoreType.DMA((row,)),
            pltpu.SemaphoreType.DMA((row,)),
            pltpu.SemaphoreType.DMA((row,)),
            pltpu.SemaphoreType.DMA((row,)),
            pltpu.SemaphoreType.DMA((18,)),
            pltpu.SemaphoreType.DMA((18,)),
        ],
        compiler_params=pltpu.CompilerParams(
            collective_id=0, has_side_effects=True, vmem_limit_bytes=48 * 2**20
        ),
        name="wind_step",
    )(
        velocity,
        pressure,
        drag_rate,
        forcing,
        site_velocity,
        site_pressure,
        site_drag,
        site_forcing,
        owners,
        sweep_counts,
        parent_cells,
        point_slots,
        point_weights.reshape(1, -1),
    )


def solution(mesh):
    placed = (
        P(None, None, "tx", "ty"),
        P(None, "tx", "ty"),
        P(None, "tx", "ty"),
        P(None, None, "tx", "ty"),
        P(None, None, None, ("tx", "ty")),
        P(None, None, ("tx", "ty")),
        P(None, None, ("tx", "ty")),
        P(None, None, None, ("tx", "ty")),
        P(),
        P(),
        P(("tx", "ty"), None),
        P(None, ("tx", "ty")),
        P(("tx", "ty")),
    )
    return jax.shard_map(
        shards,
        mesh=mesh,
        in_specs=placed,
        out_specs=(
            P(None, None, "tx", "ty"),
            P(None, "tx", "ty"),
            P(None, None, None, ("tx", "ty")),
            P(None, None, ("tx", "ty")),
        ),
        check_vma=False,
    )
```

```python
import functools

import jax
import jax.numpy as jnp
from jax import lax
from jax.experimental import pallas as pl
from jax.experimental.pallas import tpu as pltpu
from jax.sharding import PartitionSpec as P

F32 = jnp.float32
BF16 = jnp.bfloat16
MESH = pl.DeviceIdType.MESH

NZ = 48
SZ = 16
CAP = 1024
SWEEPS = 8
SSWEEPS = 6
RELAX = 0.3
SIXTH = 1.0 / 6.0
CHUNK = 512
POINTS = 4352
PCHUNK = 256
ZB = 48
FB = 16
EARLY = 4


def one_hot(key, depth):
    n = key.shape[1]
    rows = lax.broadcasted_iota(jnp.int32, (256, n), 0).astype(BF16)
    parts = []
    for b in range(depth // 256):
        low = jnp.where((key >> 8) == b, key & 255, -1) if depth > 256 else key
        low = jnp.broadcast_to(low.astype(F32).astype(BF16), (256, n))
        parts.append(jnp.where(rows == low, jnp.ones((), BF16), jnp.zeros((), BF16)))
    return jnp.concatenate(parts, axis=0) if len(parts) > 1 else parts[0]


def pieces(v):
    hi = v.astype(BF16)
    return hi, (v - hi.astype(F32)).astype(BF16)


def kernel(
    row,
    rows_tx,
    far_vel,
    far_pre,
    far_drag,
    far_forc,
    far_svel,
    far_spre,
    far_sdrag,
    far_sforc,
    owners,
    counts,
    far_cells,
    far_slots,
    far_weights,
    far_out,
    vel,
    pre,
    drag,
    forc,
    svel,
    spre,
    sdrag,
    sforc,
    cells,
    slots,
    weights,
    flat,
    nvel,
    npre,
    nsvel,
    nspre,
    sidx,
    ridx,
    table,
    rep,
    got,
    table2,
    planes,
    xs,
    xr,
    ys,
    yr,
    pred,
    pxs,
    pxr,
    pys,
    pyr,
    src,
    hs,
    hr,
    hm,
    corr,
    step,
    slope,
    sps,
    spr,
    sh,
    wes,
    wer,
    wem,
    load_sem,
    out_sem,
    idx_send,
    idx_recv,
    rep_send,
    rep_recv,
    halo_send,
    halo_recv,
):
    tx = lax.axis_index("tx")
    ty = lax.axis_index("ty")
    me = tx * row + ty
    total = row * rows_tx

    def device(a, b):
        return {"tx": a, "ty": b}

    def place(d):
        return device(d // row, lax.rem(d, row))

    x_before = device(lax.rem(tx + rows_tx - 1, rows_tx), ty)
    x_after = device(lax.rem(tx + 1, rows_tx), ty)
    y_before = device(tx, lax.rem(ty + row - 1, row))
    y_after = device(tx, lax.rem(ty + 1, row))
    d_before = place(lax.rem(me + total - 1, total))
    d_after = place(lax.rem(me + 1, total))

    loads = {}
    for n, (name, far, near) in enumerate(
        (
            ("cells", far_cells, cells),
            ("vel", far_vel, vel),
            ("pre", far_pre, pre),
            ("svel", far_svel, svel),
            ("spre", far_spre, spre),
            ("sdrag", far_sdrag, sdrag),
            ("sforc", far_sforc, sforc),
            ("drag", far_drag, drag),
            ("forc", far_forc, forc),
            ("slots", far_slots, slots),
            ("weights", far_weights, weights),
        )
    ):
        loads[name] = pltpu.make_async_copy(far, near, load_sem.at[n])
        loads[name].start()

    def loaded(*names):
        for name in names:
            loads[name].wait()

    barrier = pltpu.get_barrier_semaphore()
    for t in range(1, row):
        pl.semaphore_signal(
            barrier, inc=1, device_id=device(tx, lax.rem(ty + t, row)), device_id_type=MESH
        )
    for there in (x_before, x_after, d_before, d_after):
        pl.semaphore_signal(barrier, inc=1, device_id=there, device_id_type=MESH)

    lane = lax.broadcasted_iota(jnp.int32, (8, 128), 1)
    sub = lax.broadcasted_iota(jnp.int32, (8, 128), 0)
    zero = jnp.zeros((8, 128), F32)

    def up(v):
        return pltpu.roll(v, 1, v.ndim - 1)

    def down(v):
        return pltpu.roll(v, 127, v.ndim - 1)

    def sub_up(v):
        return pltpu.roll(v, 1, v.ndim - 2)

    def sub_down(v):
        return pltpu.roll(v, 7, v.ndim - 2)

    def copy(src_ref, dst_ref, number, there):
        return pltpu.make_async_remote_copy(
            src_ref=src_ref,
            dst_ref=dst_ref,
            send_sem=halo_send.at[number],
            recv_sem=halo_recv.at[number],
            device_id=there,
            device_id_type=MESH,
        )

    field = [vel.at[0], vel.at[1], vel.at[2], pre]

    loaded("cells")
    for p in range(row):
        sidx[p] = cells[p : p + 1, :]

    loaded("vel", "pre")
    for f in range(4):
        xs[0, f] = field[f][:, 0, :]
        xs[1, f] = field[f][:, 7, :]

    def pack_fields(zz, acc):
        acc = list(acc)
        for f in range(4):
            j = f * 16 + zz
            here = (lane >> 1) == j
            for g in range(3):
                acc[g] = jnp.where(
                    here, pltpu.roll(field[f][g * 16 + zz], 2 * j + 1, 1), acc[g]
                )
        return tuple(acc)

    acc = lax.fori_loop(0, 16, pack_fields, (zero,) * 3)
    for g in range(3):
        ys[g] = acc[g]

    sfield = [svel.at[0], svel.at[1], svel.at[2], spre, sdrag, sforc.at[0], sforc.at[1]]

    loaded("svel", "spre", "sdrag", "sforc")

    def pack_site(j, acc):
        acc = list(acc)
        here = (lane >> 4) == j
        for f in range(7):
            for g in range(2):
                acc[2 * f + g] = jnp.where(
                    here, pltpu.roll(sfield[f][g * 8 + j], 16 * j + 8, 1), acc[2 * f + g]
                )
        return tuple(acc)

    acc = lax.fori_loop(0, 8, pack_site, (zero,) * 14)
    for g in range(14):
        sps[g] = acc[g]

    pl.semaphore_wait(barrier, row - 1 + 4)

    def index_copy(to, slot):
        return pltpu.make_async_remote_copy(
            src_ref=sidx.at[to],
            dst_ref=ridx.at[ty],
            send_sem=idx_send.at[to],
            recv_sem=idx_recv.at[slot],
            device_id=device(tx, to),
            device_id_type=MESH,
        )

    for t in range(1, row):
        index_copy(lax.rem(ty + t, row), ty).start()

    fields_x = [copy(xs.at[0], xr.at[1], 0, x_before), copy(xs.at[1], xr.at[0], 1, x_after)]
    fields_y = [copy(ys, yr.at[1], 2, y_before), copy(ys, yr.at[0], 3, y_after)]
    site_y = [copy(sps, spr.at[1], 4, d_before), copy(sps, spr.at[0], 5, d_after)]
    pred_x = [copy(pxs.at[0], pxr.at[1], 6, x_before), copy(pxs.at[1], pxr.at[0], 7, x_after)]
    pred_y = [copy(pys, pyr.at[1], 8, y_before), copy(pys, pyr.at[0], 9, y_after)]
    src_y = [copy(hs, hr.at[1], 10, y_before), copy(hs, hr.at[0], 11, y_after)]
    src_x = [
        copy(src.at[:, 8:16, 0:128], src.at[:, 16:24, 0:128], 12, x_before),
        copy(src.at[:, 8:16, 0:128], src.at[:, 0:8, 0:128], 13, x_after),
    ]
    corner_x = [copy(hm.at[1], hm.at[2], 14, x_before), copy(hm.at[1], hm.at[0], 15, x_after)]
    plane_y = [copy(wes, wer.at[1], 16, d_before), copy(wes, wer.at[0], 17, d_after)]

    def start(pair):
        for c in pair:
            c.start()

    def arrive(pair):
        for c in pair:
            c.wait_recv()

    start(fields_x)
    start(fields_y)
    start(site_y)

    for f in range(4):
        for x in range(8):
            hi, lo = pieces(field[f][:, x, :])
            table[f * NZ : (f + 1) * NZ, x * 128 : (x + 1) * 128] = hi
            table[(4 + f) * NZ : (5 + f) * NZ, x * 128 : (x + 1) * 128] = lo

    def lookup(q):
        for c in range(CAP // CHUNK):
            v = ridx[q, :, c * CHUNK : (c + 1) * CHUNK]
            found = jnp.dot(table[...], one_hot(v & 1023, 1024), preferred_element_type=F32)
            layer = lax.broadcasted_iota(jnp.int32, (NZ, CHUNK), 0) == (v >> 10)
            for f in range(4):
                s = found[f * NZ : (f + 1) * NZ] + found[(4 + f) * NZ : (5 + f) * NZ]
                s = jnp.sum(jnp.where(layer, s, 0.0), axis=0, keepdims=True)
                for k in range(CHUNK // 128):
                    r = c * (CHUNK // 128) + k
                    rep[q, f, r : r + 1, :] = s[:, k * 128 : (k + 1) * 128]

    def reply_copy(to, slot):
        return pltpu.make_async_remote_copy(
            src_ref=rep.at[to],
            dst_ref=got.at[ty],
            send_sem=rep_send.at[to],
            recv_sem=rep_recv.at[slot],
            device_id=device(tx, to),
            device_id_type=MESH,
        )

    def serve(t, _):
        q = lax.rem(ty + row - t, row)
        index_copy(q, q).wait_recv()
        lookup(q)
        reply_copy(q, ty).start()
        return 0

    ridx[ty] = sidx[ty]
    lookup(ty)
    got[ty] = rep[ty]

    has_x = [jnp.where(tx > 0, 1.0, 0.0), jnp.where(tx < rows_tx - 1, 1.0, 0.0)]
    has_y = [jnp.where(ty > 0, 1.0, 0.0), jnp.where(ty < row - 1, 1.0, 0.0)]
    edge_y = jnp.where(lane < 64, has_y[0], has_y[1])

    lax.fori_loop(1, 4, serve, 0)

    loaded("drag", "forc")
    arrive(fields_x)
    arrive(fields_y)
    for g in range(3):
        first = (lane & 1) == 0
        yr[0, g] = jnp.where(first, down(yr[1, g]), up(yr[0, g]))

    def below(ref, z):
        v = ref[jnp.maximum(z - 1, 0)]
        return v * jnp.where(z > 0, 1.0, 0.0)

    def above(ref, z):
        v = ref[jnp.minimum(z + 1, NZ - 1)]
        return v * jnp.where(z < NZ - 1, 1.0, 0.0)

    def x_sides(v, low, high):
        low = jnp.broadcast_to(low, (8, 128)) * has_x[0]
        high = jnp.broadcast_to(high, (8, 128)) * has_x[1]
        return jnp.where(sub == 0, low, sub_up(v)), jnp.where(sub == 7, high, sub_down(v))

    def y_sides(v, edge):
        edge = edge * edge_y
        return jnp.where(lane == 0, edge, up(v)), jnp.where(lane == 127, edge, down(v))

    def predict(zz, packed):
        for g in range(3):
            z = g * 16 + zz
            inverse = 1.0 / (6.0 + drag[z])
            sides = []
            for f in range(4):
                v = field[f][z]
                xm, xp = x_sides(v, xr[0, f, pl.ds(z, 1), :], xr[1, f, pl.ds(z, 1), :])
                k = 2 * (f * 16 + zz) + 1
                ym, yp = y_sides(v, pltpu.roll(yr[0, g], 128 - k, 1))
                sides.append((xm, xp, ym, yp, below(field[f], z), above(field[f], z)))
            push = sides[3]
            push = [(push[1] - push[0]) * 0.5, (push[3] - push[2]) * 0.5, (push[5] - push[4]) * 0.5]
            out = []
            for i in range(3):
                s = sides[i]
                n = ((s[0] + s[1]) + (s[2] + s[3])) + (s[4] + s[5])
                if i < 2:
                    n = n + forc[i, z]
                out.append((n - push[i]) * inverse)
                pred[i, z] = out[i]
            packed = jnp.where((lane >> 1) == z, pltpu.roll(out[1], 2 * z + 1, 1), packed)
        return packed

    pys[...] = lax.fori_loop(0, 16, predict, zero)
    pxs[0] = pred[0, :, 0, :]
    pxs[1] = pred[0, :, 7, :]
    start(pred_x)
    start(pred_y)

    lax.fori_loop(4, 7, serve, 0)

    arrive(pred_x)
    arrive(pred_y)
    first = (lane & 1) == 0
    edges_v = jnp.where(first, down(pyr[1]), up(pyr[0]))

    def source(j, packed):
        packed = list(packed)
        for g in range(6):
            z = g * 8 + j
            xm, xp = x_sides(pred[0, z], pxr[0, pl.ds(z, 1), :], pxr[1, pl.ds(z, 1), :])
            ym, yp = y_sides(pred[1, z], pltpu.roll(edges_v, 127 - 2 * z, 1))
            div = (xp - xm) + (yp - ym) + (above(pred.at[2], z) - below(pred.at[2], z))
            s = div * 0.5 * (6.0 + drag[z])
            src[z, 8:16, 0:128] = s
            packed[g] = jnp.where((lane >> 4) == j, pltpu.roll(s, 16 * j + 8, 1), packed[g])
        return tuple(packed)

    acc = lax.fori_loop(0, 8, source, (zero,) * 6)
    for g in range(6):
        hs[g] = acc[g]
    start(src_y)

    lax.fori_loop(7, 10, serve, 0)

    arrive(src_y)
    left = ((lane >> 3) & 1) == 0
    for g in range(6):
        hm[1, g] = jnp.where(left, hr[0, g], hr[1, g])
    start(src_x)
    start(corner_x)

    lax.fori_loop(10, row, serve, 0)

    arrive(src_x)
    arrive(corner_x)
    inside = []
    for b in range(3):
        m = (has_x[0], 1.0, has_x[1])[b] * SIXTH
        inside.append(
            jnp.concatenate([jnp.full((8, 128), m, F32), edge_flip(lane, has_y) * m], axis=1)
        )
    inside = jnp.concatenate(inside, axis=0)[None]

    for n in range(2):
        corr[n, 0] = jnp.zeros((40, 256), F32)
        corr[n, NZ + 1] = jnp.zeros((40, 256), F32)
        corr[n, 1 : NZ + 1, 0:8, :] = jnp.zeros((NZ, 8, 256), F32)
        corr[n, 1 : NZ + 1, 32:40, :] = jnp.zeros((NZ, 8, 256), F32)

    def widen(j, _):
        for b in range(3):
            for g in range(6):
                z = g * 8 + j
                s = pltpu.roll(hm[b, g], 120 - 16 * j, 1)
                m = inside[0, 8 * b : 8 * b + 8]
                src[z, 8 * b : 8 * b + 8, 128:256] = s
                corr[1, z + 1, 8 * b + 8 : 8 * b + 16, 0:128] = (
                    -src[z, 8 * b : 8 * b + 8, 0:128] * m[:, :128]
                )
                corr[1, z + 1, 8 * b + 8 : 8 * b + 16, 128:256] = -s * m[:, 128:]
        return 0

    lax.fori_loop(0, 8, widen, 0)

    at = lax.broadcasted_iota(jnp.int32, (256, 256), 0)
    to = lax.broadcasted_iota(jnp.int32, (256, 256), 1)
    after = jnp.where(((at - to) & 255) == 1, 1.0, 0.0)
    before = jnp.where(((to - at) & 255) == 1, 1.0, 0.0)
    both = (after + before).astype(BF16)
    step[0:256, :] = both
    step[256:512, :] = both
    slope[0:256, :] = (after - before)[:, :128].astype(BF16)
    slope[256:512, :] = (after - before)[:, :128].astype(BF16)

    def apply(v, matrix):
        layers, rows, lanes = v.shape
        hi, lo = pieces(v.reshape(layers * rows, lanes))
        out = jnp.dot(
            jnp.concatenate([hi, lo], axis=1), matrix[...], preferred_element_type=F32
        )
        return out.reshape(layers, rows, out.shape[1])

    def sweep(k):
        now, later = k % 2, (k + 1) % 2
        first, rows = (0, 24) if SWEEPS - k > 4 else (4, 16)
        lo, hi = first + 8, first + 8 + rows
        for i in range(NZ // ZB):
            z = i * ZB
            n = apply(corr[now, z + 1 : z + 1 + ZB, lo:hi, :], step)
            n = n + (
                corr[now, z + 1 : z + 1 + ZB, lo - 1 : hi - 1, :]
                + corr[now, z + 1 : z + 1 + ZB, lo + 1 : hi + 1, :]
            )
            n = n + (corr[now, z : z + ZB, lo:hi, :] + corr[now, z + 2 : z + 2 + ZB, lo:hi, :])
            n = n - src[z : z + ZB, first : first + rows, :]
            corr[later, z + 1 : z + 1 + ZB, lo:hi, :] = n * inside[:, first : first + rows]

    for k in range(1, EARLY):
        sweep(k)

    loaded("slots", "weights")
    flat[...] = weights[...].reshape(1, POINTS)
    for t in range(1, row):
        q = lax.rem(ty + row - t, row)
        reply_copy(q, q).wait_recv()
    for f in range(4):
        for b in range(2):
            for u in range(row // 4):
                v = jnp.concatenate([got[4 * u + b, f], got[4 * u + 2 + b, f]], axis=0)
                hi, lo = pieces(v)
                r = f * 4 * row + u * 16
                table2[r : r + 16, b * 128 : (b + 1) * 128] = hi
                table2[16 * row + r : 16 * row + r + 16, b * 128 : (b + 1) * 128] = lo

    def point(c, _):
        at = pl.ds(pl.multiple_of(c * PCHUNK, PCHUNK), PCHUNK)
        j = jnp.concatenate([slots[0:1, at], slots[1:2, at]], axis=1)
        key = (j & 127) | (((j >> 10) & 1) << 7)
        m = ((j >> 11) << 3) | ((j >> 7) & 7)
        found = jnp.dot(table2[...], one_hot(key, 256), preferred_element_type=F32)
        here = lax.broadcasted_iota(jnp.int32, (4 * row, 2 * PCHUNK), 0) == m
        w = (2.0 * flat[:, at].astype(F32) + 1.0) * 0.125
        for f in range(4):
            r = f * 4 * row
            s = found[r : r + 4 * row] + found[16 * row + r : 16 * row + r + 4 * row]
            s = jnp.sum(jnp.where(here, s, 0.0), axis=0, keepdims=True)
            v = w * s[:, :PCHUNK] + (1.0 - w) * s[:, PCHUNK:]
            planes[f, pl.ds(2 * c, 1), :] = v[:, :128]
            planes[f, pl.ds(2 * c + 1, 1), :] = v[:, 128:]
        return 0

    lax.fori_loop(0, POINTS // PCHUNK, point, 0)

    acc = [zero, zero]
    for n in range(16):
        v = planes[n // 4, (n % 4) * 8 : (n % 4) * 8 + 8, :]
        j = n % 8
        acc[n // 8] = jnp.where((lane >> 4) == j, pltpu.roll(v, 16 * j + 8, 1), acc[n // 8])
    wes[0] = acc[0]
    wes[1] = acc[1]
    start(plane_y)

    for k in range(EARLY, SWEEPS):
        sweep(k)
    last = SWEEPS % 2

    def finish(i, _):
        z = i * FB
        c = corr[last, pl.ds(z + 1, FB), 16:24, :]
        gy = apply(c, slope)
        gx = corr[last, pl.ds(z + 1, FB), 17:25, :128] - corr[last, pl.ds(z + 1, FB), 15:23, :128]
        gz = corr[last, pl.ds(z + 2, FB), 16:24, :128] - corr[last, pl.ds(z, FB), 16:24, :128]
        half = 0.5 / (6.0 + drag[pl.ds(z, FB)])
        nvel[0, pl.ds(z, FB)] = pred[0, pl.ds(z, FB)] - gx * half
        nvel[1, pl.ds(z, FB)] = pred[1, pl.ds(z, FB)] - gy * half
        nvel[2, pl.ds(z, FB)] = pred[2, pl.ds(z, FB)] - gz * half
        npre[pl.ds(z, FB)] = pre[pl.ds(z, FB)] + RELAX * c[:, :, :128]
        return 0

    lax.fori_loop(0, NZ // FB, finish, 0)

    stores = []
    for n in range(8):
        near = (nvel.at[0], nvel.at[1], nvel.at[2], npre, nsvel.at[0], nsvel.at[1], nsvel.at[2], nspre)[n]
        first = n * NZ if n < 4 else 4 * NZ + (n - 4) * SZ
        size = NZ if n < 4 else SZ
        stores.append(pltpu.make_async_copy(near, far_out.at[first : first + size], out_sem.at[n]))
    for n in range(4):
        stores[n].start()

    own = owners[me]
    begins = (me == 0) | (owners[jnp.maximum(me - 1, 0)] != own)
    ends = (me == total - 1) | (owners[jnp.minimum(me + 1, total - 1)] != own)
    begins = jnp.full((8, 128), begins.astype(F32), F32)
    ends = jnp.full((8, 128), ends.astype(F32), F32)
    allowed = jnp.full((8, 128), counts[own], jnp.int32)
    other = jnp.where(lane < 64, ends, begins) > 0.5

    def ends_of(f):
        s = jnp.where((lane & 7) == sub, jnp.broadcast_to(planes[f, 32:33, :], (8, 128)), 0.0)
        n = jnp.where((lane & 7) == sub, jnp.broadcast_to(planes[f, 33:34, :], (8, 128)), 0.0)
        for k in (1, 2, 4):
            s = s + pltpu.roll(s, k, 1)
            n = n + pltpu.roll(n, 128 - k, 1)
        both = jnp.where((lane & 7) == 7, s, pltpu.roll(n, 8, 1))
        return [pltpu.roll(both, (120 - 8 * z) % 128, 1) for z in range(SZ)]

    outer = [jnp.stack(ends_of(f)) for f in range(4)]
    edge_lane = (lane == 0) | (lane == 127)

    def with_ends(v, f):
        return jnp.where((edge_lane & other)[None], outer[f], v)

    arrive(site_y)
    arrive(plane_y)
    left = ((lane >> 3) & 1) == 0
    for g in range(14):
        spr[0, g] = jnp.where(left, spr[0, g], spr[1, g])
    for n in range(7 * SZ):
        sh[n // SZ, n % SZ] = pltpu.roll(spr[0, n // 8], (120 - 16 * (n % 8)) % 128, 1)
    for g in range(2):
        v = jnp.where(left, wer[0, g], wer[1, g])
        for j in range(8):
            n = g * 8 + j
            wem[n // 4, (n % 4) * 8 : (n % 4) * 8 + 8, :] = pltpu.roll(v, (120 - 16 * j) % 128, 1)

    west = [[planes[f, 0:SZ, :], wem[f, 0:SZ, :]] for f in range(4)]
    east = [[planes[f, SZ : 2 * SZ, :], wem[f, SZ : 2 * SZ, :]] for f in range(4)]

    def layer_sides(v):
        blank = jnp.zeros((1, 8, 128), F32)
        return jnp.concatenate([blank, v[:-1]], axis=0), jnp.concatenate([v[1:], blank], axis=0)

    def site_x(v, h, f):
        shape = (SZ, 8, 128)
        if f is None:
            low = high = jnp.zeros(shape, F32)
        else:
            low = jnp.broadcast_to(west[f][h][:, None, :], shape)
            high = jnp.broadcast_to(east[f][h][:, None, :], shape)
        return jnp.where(sub[None] == 0, low, sub_up(v)), jnp.where(sub[None] == 7, high, sub_down(v))

    def site_y_sides(pair):
        u = [up(v) for v in pair]
        d = [down(v) for v in pair]
        return [
            (
                jnp.where(lane[None] == 0, u[1 - h], u[h]),
                jnp.where(lane[None] == 127, d[1 - h], d[h]),
            )
            for h in range(2)
        ]

    fields = [[sfield[f][...], with_ends(sh[f], f)] for f in range(4)]
    diag = [6.0 + sdrag[...], 6.0 + sh[4]]
    inverse = [1.0 / v for v in diag]
    force = [[sforc[i], sh[5 + i]] for i in range(2)]
    xside = [[site_x(fields[f][h], h, f) for h in range(2)] for f in range(4)]
    yside = [site_y_sides(fields[f]) for f in range(4)]
    moved = [[None, None] for _ in range(3)]
    for h in range(2):
        below_p, above_p = layer_sides(fields[3][h])
        push = [
            (xside[3][h][1] - xside[3][h][0]) * 0.5,
            (yside[3][h][1] - yside[3][h][0]) * 0.5,
            (above_p - below_p) * 0.5,
        ]
        for i in range(3):
            lo, hi = layer_sides(fields[i][h])
            n = (xside[i][h][0] + xside[i][h][1]) + (yside[i][h][0] + yside[i][h][1]) + (lo + hi)
            if i < 2:
                n = n + force[i][h]
            v = (n - push[i]) * inverse[h]
            moved[i][h] = with_ends(v, i) if h == 1 else v

    ys_v = site_y_sides(moved[1])
    term = []
    for h in range(2):
        xm, xp = site_x(moved[0][h], h, 0)
        lo, hi = layer_sides(moved[2][h])
        term.append(((xp - xm) + (ys_v[h][1] - ys_v[h][0]) + (hi - lo)) * 0.5 * diag[h])

    keep = [
        jnp.full((1, 8, 128), SIXTH, F32),
        jnp.where(other, 0.0, SIXTH)[None],
    ]
    e = [-term[h] * keep[h] for h in range(2)]
    for k in range(1, SSWEEPS):
        sides = site_y_sides(e)
        fresh = []
        for h in range(2):
            xm, xp = site_x(e[h], h, None)
            lo, hi = layer_sides(e[h])
            n = (xm + xp) + (sides[h][0] + sides[h][1]) + (lo + hi)
            fresh.append(jnp.where((allowed > k)[None], (n - term[h]) * keep[h], e[h]))
        e = fresh
    xm, xp = site_x(e[0], 0, None)
    ym, yp = site_y_sides(e)[0]
    lo, hi = layer_sides(e[0])
    half = 0.5 * inverse[0]
    nsvel[0] = moved[0][0] - (xp - xm) * half
    nsvel[1] = moved[1][0] - (yp - ym) * half
    nsvel[2] = moved[2][0] - (hi - lo) * half
    nspre[...] = spre[...] + RELAX * e[0]

    for n in range(4, 8):
        stores[n].start()

    for pair in (fields_x, fields_y, site_y, pred_x, pred_y, src_y, src_x, corner_x, plane_y):
        for c in pair:
            c.wait_send()
    for t in range(1, row):
        q = lax.rem(ty + t, row)
        index_copy(q, q).wait_send()
        reply_copy(q, q).wait_send()
    for c in stores:
        c.wait()


def spread(far, nvel, npre, nsvel, nspre, held, sem):
    places = (nvel.at[0], nvel.at[1], nvel.at[2], npre)
    places += (nsvel.at[0], nsvel.at[1], nsvel.at[2], nspre)
    first, moves = 0, []
    for n, place in enumerate(places):
        part = pl.ds(first, place.shape[0])
        moves.append(
            (
                pltpu.make_async_copy(far.at[part], held.at[part], sem.at[0, n]),
                pltpu.make_async_copy(held.at[part], place, sem.at[1, n]),
            )
        )
        first += place.shape[0]
    for come, _ in moves:
        come.start()
    for come, go in moves:
        come.wait()
        go.start()
    for _, go in moves:
        go.wait()


def edge_flip(lane, has_y):
    return jnp.where(lane < 64, has_y[1], has_y[0])


def shards(
    velocity,
    pressure,
    drag_rate,
    forcing,
    site_velocity,
    site_pressure,
    site_drag,
    site_forcing,
    owners,
    sweep_counts,
    parent_cells,
    point_slots,
    point_weights,
):
    row = lax.axis_size("ty")
    rows_tx = lax.axis_size("tx")
    sm = pl.BlockSpec(memory_space=pltpu.SMEM)
    hbm = pl.BlockSpec(memory_space=pl.ANY)

    def v(*shape):
        return pltpu.VMEM(shape, F32)

    both = pl.pallas_call(
        functools.partial(kernel, row, rows_tx),
        out_shape=jax.ShapeDtypeStruct((4 * (NZ + SZ), 8, 128), F32),
        in_specs=[hbm] * 8 + [sm] * 2 + [hbm] * 3,
        out_specs=hbm,
        scratch_shapes=[
            v(3, NZ, 8, 128),
            v(NZ, 8, 128),
            v(NZ, 8, 128),
            v(2, NZ, 8, 128),
            v(3, SZ, 8, 128),
            v(SZ, 8, 128),
            v(SZ, 8, 128),
            v(2, SZ, 8, 128),
            pltpu.VMEM((row, CAP), jnp.int32),
            pltpu.VMEM((2, POINTS), jnp.int32),
            pltpu.VMEM((POINTS,), jnp.int32),
            pltpu.VMEM((1, POINTS), jnp.int32),
            v(3, NZ, 8, 128),
            v(NZ, 8, 128),
            v(3, SZ, 8, 128),
            v(SZ, 8, 128),
            pltpu.VMEM((row, 1, CAP), jnp.int32),
            pltpu.VMEM((row, 1, CAP), jnp.int32),
            pltpu.VMEM((8 * NZ, 1024), BF16),
            v(row, 4, 8, 128),
            v(row, 4, 8, 128),
            pltpu.VMEM((32 * row, 256), BF16),
            v(4, 40, 128),
            v(2, 4, NZ, 128),
            v(2, 4, NZ, 128),
            v(3, 8, 128),
            v(2, 3, 8, 128),
            v(3, NZ, 8, 128),
            v(2, NZ, 128),
            v(2, NZ, 128),
            v(8, 128),
            v(2, 8, 128),
            v(NZ, 24, 256),
            v(6, 8, 128),
            v(2, 6, 8, 128),
            v(3, 6, 8, 128),
            v(2, NZ + 2, 40, 256),
            pltpu.VMEM((512, 256), BF16),
            pltpu.VMEM((512, 128), BF16),
            v(14, 8, 128),
            v(2, 14, 8, 128),
            v(7, SZ, 8, 128),
            v(2, 8, 128),
            v(2, 2, 8, 128),
            v(4, 2 * SZ, 128),
            pltpu.SemaphoreType.DMA((11,)),
            pltpu.SemaphoreType.DMA((8,)),
            pltpu.SemaphoreType.DMA((row,)),
            pltpu.SemaphoreType.DMA((row,)),
            pltpu.SemaphoreType.DMA((row,)),
            pltpu.SemaphoreType.DMA((row,)),
            pltpu.SemaphoreType.DMA((18,)),
            pltpu.SemaphoreType.DMA((18,)),
        ],
        compiler_params=pltpu.CompilerParams(
            collective_id=0, has_side_effects=True, vmem_limit_bytes=60 * 2**20
        ),
        name="wind_step",
    )(
        velocity,
        pressure,
        drag_rate,
        forcing,
        site_velocity,
        site_pressure,
        site_drag,
        site_forcing,
        owners,
        sweep_counts,
        parent_cells,
        point_slots,
        point_weights,
    )
    return pl.pallas_call(
        spread,
        out_shape=[
            jax.ShapeDtypeStruct(a.shape, F32)
            for a in (velocity, pressure, site_velocity, site_pressure)
        ],
        in_specs=[hbm],
        out_specs=[hbm] * 4,
        scratch_shapes=[v(4 * (NZ + SZ), 8, 128), pltpu.SemaphoreType.DMA((2, 8))],
        name="spread",
    )(both)


def solution(mesh):
    placed = (
        P(None, None, "tx", "ty"),
        P(None, "tx", "ty"),
        P(None, "tx", "ty"),
        P(None, None, "tx", "ty"),
        P(None, None, None, ("tx", "ty")),
        P(None, None, ("tx", "ty")),
        P(None, None, ("tx", "ty")),
        P(None, None, None, ("tx", "ty")),
        P(),
        P(),
        P(("tx", "ty"), None),
        P(None, ("tx", "ty")),
        P(("tx", "ty")),
    )
    return jax.shard_map(
        shards,
        mesh=mesh,
        in_specs=placed,
        out_specs=(
            P(None, None, "tx", "ty"),
            P(None, "tx", "ty"),
            P(None, None, None, ("tx", "ty")),
            P(None, None, ("tx", "ty")),
        ),
        check_vma=False,
    )
```

```python
import functools

import jax
import jax.numpy as jnp
from jax import lax
from jax.experimental import pallas as pl
from jax.experimental.pallas import tpu as pltpu
from jax.sharding import PartitionSpec as P

F32 = jnp.float32
BF16 = jnp.bfloat16
MESH = pl.DeviceIdType.MESH

NZ = 48
SZ = 16
CAP = 1024
SWEEPS = 8
SSWEEPS = 6
RELAX = 0.3
SIXTH = 1.0 / 6.0
CHUNK = 512
POINTS = 4352
PCHUNK = 256
ZB = 48
FB = 16
EARLY = 5


def one_hot(key, depth):
    n = key.shape[1]
    rows = lax.broadcasted_iota(jnp.int32, (256, n), 0).astype(BF16)
    parts = []
    for b in range(depth // 256):
        low = jnp.where((key >> 8) == b, key & 255, -1) if depth > 256 else key
        low = jnp.broadcast_to(low.astype(F32).astype(BF16), (256, n))
        parts.append(jnp.where(rows == low, jnp.ones((), BF16), jnp.zeros((), BF16)))
    return jnp.concatenate(parts, axis=0) if len(parts) > 1 else parts[0]


def pieces(v):
    hi = v.astype(BF16)
    return hi, (v - hi.astype(F32)).astype(BF16)


def kernel(
    row,
    rows_tx,
    far_vel,
    far_pre,
    far_drag,
    far_forc,
    far_svel,
    far_spre,
    far_sdrag,
    far_sforc,
    owners,
    counts,
    far_cells,
    far_slots,
    far_weights,
    far_out,
    vel,
    pre,
    drag,
    forc,
    svel,
    spre,
    sdrag,
    sforc,
    cells,
    slots,
    weights,
    flat,
    nvel,
    npre,
    nsvel,
    nspre,
    sidx,
    ridx,
    table,
    rep,
    got,
    table2,
    planes,
    xs,
    xr,
    ys,
    yr,
    pred,
    pxs,
    pxr,
    pys,
    pyr,
    src,
    hs,
    hr,
    hd,
    hm,
    corr,
    step,
    slope,
    sps,
    spr,
    sh,
    wes,
    wer,
    wem,
    rows,
    rim,
    load_sem,
    out_sem,
    idx_send,
    idx_recv,
    rep_send,
    rep_recv,
    halo_send,
    halo_recv,
):
    tx = lax.axis_index("tx")
    ty = lax.axis_index("ty")
    me = tx * row + ty
    total = row * rows_tx

    def device(a, b):
        return {"tx": a, "ty": b}

    def place(d):
        return device(d // row, lax.rem(d, row))

    x_before = device(lax.rem(tx + rows_tx - 1, rows_tx), ty)
    x_after = device(lax.rem(tx + 1, rows_tx), ty)
    y_before = device(tx, lax.rem(ty + row - 1, row))
    y_after = device(tx, lax.rem(ty + 1, row))
    d_before = place(lax.rem(me + total - 1, total))
    d_after = place(lax.rem(me + 1, total))

    loads = {}
    for n, (name, far, near) in enumerate(
        (
            ("cells", far_cells, cells),
            ("vel", far_vel, vel),
            ("pre", far_pre, pre),
            ("svel", far_svel, svel),
            ("spre", far_spre, spre),
            ("sdrag", far_sdrag, sdrag),
            ("sforc", far_sforc, sforc),
            ("drag", far_drag, drag),
            ("forc", far_forc, forc),
            ("slots", far_slots, slots),
            ("weights", far_weights, weights),
        )
    ):
        loads[name] = pltpu.make_async_copy(far, near, load_sem.at[n])
        loads[name].start()

    def loaded(*names):
        for name in names:
            loads[name].wait()

    diagonal = [
        device(there["tx"], side["ty"])
        for there in (x_before, x_after)
        for side in (y_before, y_after)
    ]

    barrier = pltpu.get_barrier_semaphore()
    for t in range(1, row):
        pl.semaphore_signal(
            barrier, inc=1, device_id=device(tx, lax.rem(ty + t, row)), device_id_type=MESH
        )
    for there in (x_before, x_after, d_before, d_after, *diagonal):
        pl.semaphore_signal(barrier, inc=1, device_id=there, device_id_type=MESH)

    lane = lax.broadcasted_iota(jnp.int32, (8, 128), 1)
    sub = lax.broadcasted_iota(jnp.int32, (8, 128), 0)
    zero = jnp.zeros((8, 128), F32)
    left = ((lane >> 3) & 1) == 0

    def up(v):
        return pltpu.roll(v, 1, v.ndim - 1)

    def down(v):
        return pltpu.roll(v, 127, v.ndim - 1)

    def sub_up(v):
        return pltpu.roll(v, 1, v.ndim - 2)

    def sub_down(v):
        return pltpu.roll(v, 7, v.ndim - 2)

    def copy(src_ref, dst_ref, number, there):
        return pltpu.make_async_remote_copy(
            src_ref=src_ref,
            dst_ref=dst_ref,
            send_sem=halo_send.at[number],
            recv_sem=halo_recv.at[number],
            device_id=there,
            device_id_type=MESH,
        )

    field = [vel.at[0], vel.at[1], vel.at[2], pre]

    loaded("cells")
    for p in range(row):
        sidx[p] = cells[p : p + 1, :]

    loaded("vel", "pre")
    for f in range(4):
        xs[0, f] = field[f][:, 0, :]
        xs[1, f] = field[f][:, 7, :]

    def pack_fields(zz, acc):
        acc = list(acc)
        for f in range(4):
            j = f * 16 + zz
            here = (lane >> 1) == j
            for g in range(3):
                acc[g] = jnp.where(
                    here, pltpu.roll(field[f][g * 16 + zz], 2 * j + 1, 1), acc[g]
                )
        return tuple(acc)

    acc = lax.fori_loop(0, 16, pack_fields, (zero,) * 3)
    for g in range(3):
        ys[g] = acc[g]

    sfield = [svel.at[0], svel.at[1], svel.at[2], spre, sdrag, sforc.at[0], sforc.at[1]]

    loaded("svel", "spre", "sdrag", "sforc")

    def pack_site(j, acc):
        acc = list(acc)
        here = (lane >> 4) == j
        for f in range(7):
            for g in range(2):
                acc[2 * f + g] = jnp.where(
                    here, pltpu.roll(sfield[f][g * 8 + j], 16 * j + 8, 1), acc[2 * f + g]
                )
        return tuple(acc)

    acc = lax.fori_loop(0, 8, pack_site, (zero,) * 14)
    for g in range(14):
        sps[g] = acc[g]

    pl.semaphore_wait(barrier, row - 1 + 8)

    def index_copy(to, slot):
        return pltpu.make_async_remote_copy(
            src_ref=sidx.at[to],
            dst_ref=ridx.at[ty],
            send_sem=idx_send.at[to],
            recv_sem=idx_recv.at[slot],
            device_id=device(tx, to),
            device_id_type=MESH,
        )

    for t in range(1, row):
        index_copy(lax.rem(ty + t, row), ty).start()

    fields_x = [copy(xs.at[0], xr.at[1], 0, x_before), copy(xs.at[1], xr.at[0], 1, x_after)]
    fields_y = [copy(ys, yr.at[1], 2, y_before), copy(ys, yr.at[0], 3, y_after)]
    site_y = [copy(sps, spr.at[1], 4, d_before), copy(sps, spr.at[0], 5, d_after)]
    pred_x = [copy(pxs.at[0], pxr.at[1], 6, x_before), copy(pxs.at[1], pxr.at[0], 7, x_after)]
    pred_y = [copy(pys, pyr.at[1], 8, y_before), copy(pys, pyr.at[0], 9, y_after)]
    src_y = [copy(hs, hr.at[1], 10, y_before), copy(hs, hr.at[0], 11, y_after)]
    src_x = [
        copy(src.at[:, 8:16, 0:128], src.at[:, 16:24, 0:128], 12, x_before),
        copy(src.at[:, 8:16, 0:128], src.at[:, 0:8, 0:128], 13, x_after),
    ]
    corner_x = [
        copy(hs, hd.at[1 - n // 2, 1 - n % 2], 14 + n, diagonal[n]) for n in range(4)
    ]
    plane_y = [copy(wes, wer.at[1], 18, d_before), copy(wes, wer.at[0], 19, d_after)]

    def start(pair):
        for c in pair:
            c.start()

    def arrive(pair):
        for c in pair:
            c.wait_recv()

    start(fields_x)
    start(fields_y)
    start(site_y)

    for f in range(4):
        for u in range(NZ // 16):
            for k in range(8):
                z = 16 * u + k
                hi, lo = pieces(jnp.concatenate([field[f][z], field[f][z + 8]], axis=0))
                r = f * NZ + 16 * u
                table[r : r + 16, k * 128 : (k + 1) * 128] = hi
                table[4 * NZ + r : 4 * NZ + r + 16, k * 128 : (k + 1) * 128] = lo

    def lookup(q):
        for c in range(CAP // CHUNK):
            v = ridx[q, :, c * CHUNK : (c + 1) * CHUNK]
            key = (v & 127) | (((v >> 10) & 7) << 7)
            m = ((v >> 13) << 3) | ((v >> 7) & 7)
            found = jnp.dot(table[...], one_hot(key, 1024), preferred_element_type=F32)
            layer = lax.broadcasted_iota(jnp.int32, (NZ, CHUNK), 0) == m
            for f in range(4):
                s = found[f * NZ : (f + 1) * NZ] + found[(4 + f) * NZ : (5 + f) * NZ]
                s = jnp.sum(jnp.where(layer, s, 0.0), axis=0, keepdims=True)
                for k in range(CHUNK // 128):
                    r = c * (CHUNK // 128) + k
                    rep[q, f, r : r + 1, :] = s[:, k * 128 : (k + 1) * 128]

    def reply_copy(to, slot):
        return pltpu.make_async_remote_copy(
            src_ref=rep.at[to],
            dst_ref=got.at[ty],
            send_sem=rep_send.at[to],
            recv_sem=rep_recv.at[slot],
            device_id=device(tx, to),
            device_id_type=MESH,
        )

    def serve(t, _):
        q = lax.rem(ty + row - t, row)
        index_copy(q, q).wait_recv()
        lookup(q)
        reply_copy(q, ty).start()
        return 0

    ridx[ty] = sidx[ty]
    lookup(ty)
    got[ty] = rep[ty]

    def open_site():
        for g in range(14):
            spr[0, g] = jnp.where(left, spr[0, g], spr[1, g])
        for n in range(7 * SZ):
            sh[n // SZ, n % SZ] = pltpu.roll(spr[0, n // 8], (120 - 16 * (n % 8)) % 128, 1)

    def open_slots():
        loaded("slots", "weights")
        flat[...] = weights[...].reshape(1, POINTS)
        for n in range(2 * SZ):
            at = pl.ds(n * 128, 128)
            rows[0, n : n + 1, :] = slots[0:1, at]
            rows[1, n : n + 1, :] = slots[1:2, at]
            rows[2, n : n + 1, :] = flat[:, at]
        for r in range(3):
            v = jnp.zeros((8, 128), jnp.int32)
            for g in range(4):
                v = jnp.where(
                    (lane >> 4) == g, pltpu.roll(rows[r, 8 * g : 8 * g + 8, :], 16 * g + 8, 1), v
                )
            rim[r] = v

    has_x = [jnp.where(tx > 0, 1.0, 0.0), jnp.where(tx < rows_tx - 1, 1.0, 0.0)]
    has_y = [jnp.where(ty > 0, 1.0, 0.0), jnp.where(ty < row - 1, 1.0, 0.0)]
    edge_y = jnp.where(lane < 64, has_y[0], has_y[1])

    lax.fori_loop(1, 3, serve, 0)

    loaded("drag", "forc")
    arrive(fields_x)
    arrive(fields_y)
    for g in range(3):
        first = (lane & 1) == 0
        yr[0, g] = jnp.where(first, down(yr[1, g]), up(yr[0, g]))

    def below(ref, z):
        v = ref[jnp.maximum(z - 1, 0)]
        return v * jnp.where(z > 0, 1.0, 0.0)

    def above(ref, z):
        v = ref[jnp.minimum(z + 1, NZ - 1)]
        return v * jnp.where(z < NZ - 1, 1.0, 0.0)

    def x_sides(v, low, high):
        low = jnp.broadcast_to(low, (8, 128)) * has_x[0]
        high = jnp.broadcast_to(high, (8, 128)) * has_x[1]
        return jnp.where(sub == 0, low, sub_up(v)), jnp.where(sub == 7, high, sub_down(v))

    def y_sides(v, edge):
        edge = edge * edge_y
        return jnp.where(lane == 0, edge, up(v)), jnp.where(lane == 127, edge, down(v))

    def predict(zz, packed):
        for g in range(3):
            z = g * 16 + zz
            inverse = 1.0 / (6.0 + drag[z])
            sides = []
            for f in range(4):
                v = field[f][z]
                xm, xp = x_sides(v, xr[0, f, pl.ds(z, 1), :], xr[1, f, pl.ds(z, 1), :])
                k = 2 * (f * 16 + zz) + 1
                ym, yp = y_sides(v, pltpu.roll(yr[0, g], 128 - k, 1))
                sides.append((xm, xp, ym, yp, below(field[f], z), above(field[f], z)))
            push = sides[3]
            push = [(push[1] - push[0]) * 0.5, (push[3] - push[2]) * 0.5, (push[5] - push[4]) * 0.5]
            out = []
            for i in range(3):
                s = sides[i]
                n = ((s[0] + s[1]) + (s[2] + s[3])) + (s[4] + s[5])
                if i < 2:
                    n = n + forc[i, z]
                out.append((n - push[i]) * inverse)
                pred[i, z] = out[i]
            packed = jnp.where((lane >> 1) == z, pltpu.roll(out[1], 2 * z + 1, 1), packed)
        return packed

    def serve_predict(i, packed):
        serve(3 + i, 0)
        for zz in range(8):
            packed = predict(i * 8 + zz, packed)
        return packed

    pys[...] = lax.fori_loop(0, 2, serve_predict, zero)
    pxs[0] = pred[0, :, 0, :]
    pxs[1] = pred[0, :, 7, :]
    start(pred_x)
    start(pred_y)

    lax.fori_loop(5, 8, serve, 0)

    arrive(pred_x)
    arrive(pred_y)
    first = (lane & 1) == 0
    edges_v = jnp.where(first, down(pyr[1]), up(pyr[0]))

    def source(j, packed):
        packed = list(packed)
        for g in range(6):
            z = g * 8 + j
            xm, xp = x_sides(pred[0, z], pxr[0, pl.ds(z, 1), :], pxr[1, pl.ds(z, 1), :])
            ym, yp = y_sides(pred[1, z], pltpu.roll(edges_v, 127 - 2 * z, 1))
            div = (xp - xm) + (yp - ym) + (above(pred.at[2], z) - below(pred.at[2], z))
            s = div * 0.5 * (6.0 + drag[z])
            src[z, 8:16, 0:128] = s
            packed[g] = jnp.where((lane >> 4) == j, pltpu.roll(s, 16 * j + 8, 1), packed[g])
        return tuple(packed)

    serve(8, 0)
    acc = (zero,) * 6
    for j in range(8):
        acc = source(j, acc)
    for g in range(6):
        hs[g] = acc[g]
    start(src_y)
    start(corner_x)
    start(src_x)

    serve(9, 0)
    open_slots()
    serve(10, 0)
    arrive(site_y)
    serve(11, 0)
    open_site()
    serve(12, 0)

    arrive(src_y)
    arrive(corner_x)
    for g in range(6):
        hm[0, g] = jnp.where(left, hd[0, 0, g], hd[0, 1, g])
        hm[1, g] = jnp.where(left, hr[0, g], hr[1, g])
        hm[2, g] = jnp.where(left, hd[1, 0, g], hd[1, 1, g])

    arrive(src_x)
    inside = []
    for b in range(3):
        m = (has_x[0], 1.0, has_x[1])[b] * SIXTH
        inside.append(
            jnp.concatenate([jnp.full((8, 128), m, F32), edge_flip(lane, has_y) * m], axis=1)
        )
    inside = jnp.concatenate(inside, axis=0)[None]

    for n in range(2):
        corr[n, 0] = jnp.zeros((40, 256), F32)
        corr[n, NZ + 1] = jnp.zeros((40, 256), F32)
        corr[n, 1 : NZ + 1, 0:8, :] = jnp.zeros((NZ, 8, 256), F32)
        corr[n, 1 : NZ + 1, 32:40, :] = jnp.zeros((NZ, 8, 256), F32)

    def widen(j, _):
        for b in range(3):
            for g in range(6):
                z = g * 8 + j
                s = pltpu.roll(hm[b, g], 120 - 16 * j, 1)
                m = inside[0, 8 * b : 8 * b + 8]
                src[z, 8 * b : 8 * b + 8, 128:256] = s
                corr[1, z + 1, 8 * b + 8 : 8 * b + 16, 0:128] = (
                    -src[z, 8 * b : 8 * b + 8, 0:128] * m[:, :128]
                )
                corr[1, z + 1, 8 * b + 8 : 8 * b + 16, 128:256] = -s * m[:, 128:]
        return 0

    serve(13, 0)
    for j in range(8):
        widen(j, 0)
    lax.fori_loop(14, row, serve, 0)

    at = lax.broadcasted_iota(jnp.int32, (256, 256), 0)
    to = lax.broadcasted_iota(jnp.int32, (256, 256), 1)
    after = jnp.where(((at - to) & 255) == 1, 1.0, 0.0)
    before = jnp.where(((to - at) & 255) == 1, 1.0, 0.0)
    both = (after + before).astype(BF16)
    step[0:256, :] = both
    step[256:512, :] = both
    slope[0:256, :] = (after - before)[:, :128].astype(BF16)
    slope[256:512, :] = (after - before)[:, :128].astype(BF16)

    def apply(v, matrix):
        layers, rows, lanes = v.shape
        hi, lo = pieces(v.reshape(layers * rows, lanes))
        out = jnp.dot(
            jnp.concatenate([hi, lo], axis=1), matrix[...], preferred_element_type=F32
        )
        return out.reshape(layers, rows, out.shape[1])

    def sweep(k):
        now, later = k % 2, (k + 1) % 2
        first, rows = (0, 24) if SWEEPS - k > 4 else (4, 16)
        lo, hi = first + 8, first + 8 + rows
        for i in range(NZ // ZB):
            z = i * ZB
            n = apply(corr[now, z + 1 : z + 1 + ZB, lo:hi, :], step)
            n = n + (
                corr[now, z + 1 : z + 1 + ZB, lo - 1 : hi - 1, :]
                + corr[now, z + 1 : z + 1 + ZB, lo + 1 : hi + 1, :]
            )
            n = n + (corr[now, z : z + ZB, lo:hi, :] + corr[now, z + 2 : z + 2 + ZB, lo:hi, :])
            n = n - src[z : z + ZB, first : first + rows, :]
            corr[later, z + 1 : z + 1 + ZB, lo:hi, :] = n * inside[:, first : first + rows]

    for k in range(1, EARLY):
        sweep(k)

    for t in range(1, row):
        q = lax.rem(ty + row - t, row)
        reply_copy(q, q).wait_recv()
    for f in range(4):
        for b in range(2):
            for u in range(row // 4):
                v = jnp.concatenate([got[4 * u + b, f], got[4 * u + 2 + b, f]], axis=0)
                hi, lo = pieces(v)
                r = f * 4 * row + u * 16
                table2[r : r + 16, b * 128 : (b + 1) * 128] = hi
                table2[16 * row + r : 16 * row + r + 16, b * 128 : (b + 1) * 128] = lo

    def point(j, w):
        n = w.shape[1]
        key = (j & 127) | (((j >> 10) & 1) << 7)
        m = ((j >> 11) << 3) | ((j >> 7) & 7)
        found = jnp.dot(table2[...], one_hot(key, 256), preferred_element_type=F32)
        here = lax.broadcasted_iota(jnp.int32, (4 * row, 2 * n), 0) == m
        w = (2.0 * w.astype(F32) + 1.0) * 0.125
        out = []
        for f in range(4):
            r = f * 4 * row
            s = found[r : r + 4 * row] + found[16 * row + r : 16 * row + r + 4 * row]
            s = jnp.sum(jnp.where(here, s, 0.0), axis=0, keepdims=True)
            out.append(w * s[:, :n] + (1.0 - w) * s[:, n:])
        return out

    for c in range(4):
        r = [rim[k, 2 * c + i : 2 * c + i + 1, :] for k in range(3) for i in range(2)]
        out = point(jnp.concatenate(r[:4], axis=1), jnp.concatenate(r[4:], axis=1))
        for f in range(4):
            wes[f, 2 * c : 2 * c + 1, :] = out[f][:, :128]
            wes[f, 2 * c + 1 : 2 * c + 2, :] = out[f][:, 128:]
    start(plane_y)

    for c in range(POINTS // PCHUNK):
        at = pl.ds(c * PCHUNK, PCHUNK)
        out = point(jnp.concatenate([slots[0:1, at], slots[1:2, at]], axis=1), flat[:, at])
        for f in range(4):
            planes[f, 2 * c : 2 * c + 1, :] = out[f][:, :128]
            planes[f, 2 * c + 1 : 2 * c + 2, :] = out[f][:, 128:]
    sweep(EARLY)

    for k in range(EARLY + 1, SWEEPS):
        sweep(k)
    last = SWEEPS % 2

    def finish(i, _):
        z = i * FB
        c = corr[last, pl.ds(z + 1, FB), 16:24, :]
        gy = apply(c, slope)
        gx = corr[last, pl.ds(z + 1, FB), 17:25, :128] - corr[last, pl.ds(z + 1, FB), 15:23, :128]
        gz = corr[last, pl.ds(z + 2, FB), 16:24, :128] - corr[last, pl.ds(z, FB), 16:24, :128]
        half = 0.5 / (6.0 + drag[pl.ds(z, FB)])
        nvel[0, pl.ds(z, FB)] = pred[0, pl.ds(z, FB)] - gx * half
        nvel[1, pl.ds(z, FB)] = pred[1, pl.ds(z, FB)] - gy * half
        nvel[2, pl.ds(z, FB)] = pred[2, pl.ds(z, FB)] - gz * half
        npre[pl.ds(z, FB)] = pre[pl.ds(z, FB)] + RELAX * c[:, :, :128]
        return 0

    lax.fori_loop(0, NZ // FB, finish, 0)

    stores = []
    for n in range(8):
        near = (nvel.at[0], nvel.at[1], nvel.at[2], npre, nsvel.at[0], nsvel.at[1], nsvel.at[2], nspre)[n]
        first = n * NZ if n < 4 else 4 * NZ + (n - 4) * SZ
        size = NZ if n < 4 else SZ
        stores.append(pltpu.make_async_copy(near, far_out.at[first : first + size], out_sem.at[n]))
    for n in range(4):
        stores[n].start()

    own = owners[me]
    begins = (me == 0) | (owners[jnp.maximum(me - 1, 0)] != own)
    ends = (me == total - 1) | (owners[jnp.minimum(me + 1, total - 1)] != own)
    begins = jnp.full((8, 128), begins.astype(F32), F32)
    ends = jnp.full((8, 128), ends.astype(F32), F32)
    allowed = jnp.full((8, 128), counts[own], jnp.int32)
    other = jnp.where(lane < 64, ends, begins) > 0.5

    def ends_of(f):
        s = jnp.where((lane & 7) == sub, jnp.broadcast_to(planes[f, 32:33, :], (8, 128)), 0.0)
        n = jnp.where((lane & 7) == sub, jnp.broadcast_to(planes[f, 33:34, :], (8, 128)), 0.0)
        for k in (1, 2, 4):
            s = s + pltpu.roll(s, k, 1)
            n = n + pltpu.roll(n, 128 - k, 1)
        both = jnp.where((lane & 7) == 7, s, pltpu.roll(n, 8, 1))
        return [pltpu.roll(both, (120 - 8 * z) % 128, 1) for z in range(SZ)]

    outer = [jnp.stack(ends_of(f)) for f in range(4)]
    edge_lane = (lane == 0) | (lane == 127)

    def with_ends(v, f):
        return jnp.where((edge_lane & other)[None], outer[f], v)

    arrive(plane_y)
    for f in range(4):
        v = jnp.where(left, wer[0, f], wer[1, f])
        for g in range(4):
            wem[f, 8 * g : 8 * g + 8, :] = pltpu.roll(v, 120 - 16 * g, 1)

    west = [[planes[f, 0:SZ, :], wem[f, 0:SZ, :]] for f in range(4)]
    east = [[planes[f, SZ : 2 * SZ, :], wem[f, SZ : 2 * SZ, :]] for f in range(4)]

    def layer_sides(v):
        blank = jnp.zeros((1, 8, 128), F32)
        return jnp.concatenate([blank, v[:-1]], axis=0), jnp.concatenate([v[1:], blank], axis=0)

    def site_x(v, h, f):
        shape = (SZ, 8, 128)
        if f is None:
            low = high = jnp.zeros(shape, F32)
        else:
            low = jnp.broadcast_to(west[f][h][:, None, :], shape)
            high = jnp.broadcast_to(east[f][h][:, None, :], shape)
        return jnp.where(sub[None] == 0, low, sub_up(v)), jnp.where(sub[None] == 7, high, sub_down(v))

    def site_y_sides(pair):
        u = [up(v) for v in pair]
        d = [down(v) for v in pair]
        return [
            (
                jnp.where(lane[None] == 0, u[1 - h], u[h]),
                jnp.where(lane[None] == 127, d[1 - h], d[h]),
            )
            for h in range(2)
        ]

    fields = [[sfield[f][...], with_ends(sh[f], f)] for f in range(4)]
    diag = [6.0 + sdrag[...], 6.0 + sh[4]]
    inverse = [1.0 / v for v in diag]
    force = [[sforc[i], sh[5 + i]] for i in range(2)]
    xside = [[site_x(fields[f][h], h, f) for h in range(2)] for f in range(4)]
    yside = [site_y_sides(fields[f]) for f in range(4)]
    moved = [[None, None] for _ in range(3)]
    for h in range(2):
        below_p, above_p = layer_sides(fields[3][h])
        push = [
            (xside[3][h][1] - xside[3][h][0]) * 0.5,
            (yside[3][h][1] - yside[3][h][0]) * 0.5,
            (above_p - below_p) * 0.5,
        ]
        for i in range(3):
            lo, hi = layer_sides(fields[i][h])
            n = (xside[i][h][0] + xside[i][h][1]) + (yside[i][h][0] + yside[i][h][1]) + (lo + hi)
            if i < 2:
                n = n + force[i][h]
            v = (n - push[i]) * inverse[h]
            moved[i][h] = with_ends(v, i) if h == 1 else v

    ys_v = site_y_sides(moved[1])
    term = []
    for h in range(2):
        xm, xp = site_x(moved[0][h], h, 0)
        lo, hi = layer_sides(moved[2][h])
        term.append(((xp - xm) + (ys_v[h][1] - ys_v[h][0]) + (hi - lo)) * 0.5 * diag[h])

    keep = [
        jnp.full((1, 8, 128), SIXTH, F32),
        jnp.where(other, 0.0, SIXTH)[None],
    ]
    e = [-term[h] * keep[h] for h in range(2)]
    for k in range(1, SSWEEPS):
        sides = site_y_sides(e)
        fresh = []
        for h in range(2):
            xm, xp = site_x(e[h], h, None)
            lo, hi = layer_sides(e[h])
            n = (xm + xp) + (sides[h][0] + sides[h][1]) + (lo + hi)
            fresh.append(jnp.where((allowed > k)[None], (n - term[h]) * keep[h], e[h]))
        e = fresh
    xm, xp = site_x(e[0], 0, None)
    ym, yp = site_y_sides(e)[0]
    lo, hi = layer_sides(e[0])
    half = 0.5 * inverse[0]
    nsvel[0] = moved[0][0] - (xp - xm) * half
    nsvel[1] = moved[1][0] - (yp - ym) * half
    nsvel[2] = moved[2][0] - (hi - lo) * half
    nspre[...] = spre[...] + RELAX * e[0]

    for n in range(4, 8):
        stores[n].start()

    for pair in (fields_x, fields_y, site_y, pred_x, pred_y, src_y, src_x, corner_x, plane_y):
        for c in pair:
            c.wait_send()
    for t in range(1, row):
        q = lax.rem(ty + t, row)
        index_copy(q, q).wait_send()
        reply_copy(q, q).wait_send()
    for c in stores:
        c.wait()


def spread(far, nvel, npre, nsvel, nspre, held, sem):
    places = (nvel.at[0], nvel.at[1], nvel.at[2], npre)
    places += (nsvel.at[0], nsvel.at[1], nsvel.at[2], nspre)
    first, moves = 0, []
    for n, place in enumerate(places):
        part = pl.ds(first, place.shape[0])
        moves.append(
            (
                pltpu.make_async_copy(far.at[part], held.at[part], sem.at[0, n]),
                pltpu.make_async_copy(held.at[part], place, sem.at[1, n]),
            )
        )
        first += place.shape[0]
    for come, _ in moves:
        come.start()
    for come, go in moves:
        come.wait()
        go.start()
    for _, go in moves:
        go.wait()


def edge_flip(lane, has_y):
    return jnp.where(lane < 64, has_y[1], has_y[0])


def shards(
    velocity,
    pressure,
    drag_rate,
    forcing,
    site_velocity,
    site_pressure,
    site_drag,
    site_forcing,
    owners,
    sweep_counts,
    parent_cells,
    point_slots,
    point_weights,
):
    row = lax.axis_size("ty")
    rows_tx = lax.axis_size("tx")
    sm = pl.BlockSpec(memory_space=pltpu.SMEM)
    hbm = pl.BlockSpec(memory_space=pl.ANY)

    def v(*shape):
        return pltpu.VMEM(shape, F32)

    both = pl.pallas_call(
        functools.partial(kernel, row, rows_tx),
        out_shape=jax.ShapeDtypeStruct((4 * (NZ + SZ), 8, 128), F32),
        in_specs=[hbm] * 8 + [sm] * 2 + [hbm] * 3,
        out_specs=hbm,
        scratch_shapes=[
            v(3, NZ, 8, 128),
            v(NZ, 8, 128),
            v(NZ, 8, 128),
            v(2, NZ, 8, 128),
            v(3, SZ, 8, 128),
            v(SZ, 8, 128),
            v(SZ, 8, 128),
            v(2, SZ, 8, 128),
            pltpu.VMEM((row, CAP), jnp.int32),
            pltpu.VMEM((2, POINTS), jnp.int32),
            pltpu.VMEM((POINTS,), jnp.int32),
            pltpu.VMEM((1, POINTS), jnp.int32),
            v(3, NZ, 8, 128),
            v(NZ, 8, 128),
            v(3, SZ, 8, 128),
            v(SZ, 8, 128),
            pltpu.VMEM((row, 1, CAP), jnp.int32),
            pltpu.VMEM((row, 1, CAP), jnp.int32),
            pltpu.VMEM((8 * NZ, 1024), BF16),
            v(row, 4, 8, 128),
            v(row, 4, 8, 128),
            pltpu.VMEM((32 * row, 256), BF16),
            v(4, 40, 128),
            v(2, 4, NZ, 128),
            v(2, 4, NZ, 128),
            v(3, 8, 128),
            v(2, 3, 8, 128),
            v(3, NZ, 8, 128),
            v(2, NZ, 128),
            v(2, NZ, 128),
            v(8, 128),
            v(2, 8, 128),
            v(NZ, 24, 256),
            v(6, 8, 128),
            v(2, 6, 8, 128),
            v(2, 2, 6, 8, 128),
            v(3, 6, 8, 128),
            v(2, NZ + 2, 40, 256),
            pltpu.VMEM((512, 256), BF16),
            pltpu.VMEM((512, 128), BF16),
            v(14, 8, 128),
            v(2, 14, 8, 128),
            v(7, SZ, 8, 128),
            v(4, 8, 128),
            v(2, 4, 8, 128),
            v(4, 2 * SZ, 128),
            pltpu.VMEM((3, 2 * SZ, 128), jnp.int32),
            pltpu.VMEM((3, 8, 128), jnp.int32),
            pltpu.SemaphoreType.DMA((11,)),
            pltpu.SemaphoreType.DMA((8,)),
            pltpu.SemaphoreType.DMA((row,)),
            pltpu.SemaphoreType.DMA((row,)),
            pltpu.SemaphoreType.DMA((row,)),
            pltpu.SemaphoreType.DMA((row,)),
            pltpu.SemaphoreType.DMA((20,)),
            pltpu.SemaphoreType.DMA((20,)),
        ],
        compiler_params=pltpu.CompilerParams(
            collective_id=0, has_side_effects=True, vmem_limit_bytes=60 * 2**20
        ),
        name="wind_step",
    )(
        velocity,
        pressure,
        drag_rate,
        forcing,
        site_velocity,
        site_pressure,
        site_drag,
        site_forcing,
        owners,
        sweep_counts,
        parent_cells,
        point_slots,
        point_weights,
    )
    return pl.pallas_call(
        spread,
        out_shape=[
            jax.ShapeDtypeStruct(a.shape, F32)
            for a in (velocity, pressure, site_velocity, site_pressure)
        ],
        in_specs=[hbm],
        out_specs=[hbm] * 4,
        scratch_shapes=[v(4 * (NZ + SZ), 8, 128), pltpu.SemaphoreType.DMA((2, 8))],
        name="spread",
    )(both)


def solution(mesh):
    placed = (
        P(None, None, "tx", "ty"),
        P(None, "tx", "ty"),
        P(None, "tx", "ty"),
        P(None, None, "tx", "ty"),
        P(None, None, None, ("tx", "ty")),
        P(None, None, ("tx", "ty")),
        P(None, None, ("tx", "ty")),
        P(None, None, None, ("tx", "ty")),
        P(),
        P(),
        P(("tx", "ty"), None),
        P(None, ("tx", "ty")),
        P(("tx", "ty")),
    )
    return jax.shard_map(
        shards,
        mesh=mesh,
        in_specs=placed,
        out_specs=(
            P(None, None, "tx", "ty"),
            P(None, "tx", "ty"),
            P(None, None, None, ("tx", "ty")),
            P(None, None, ("tx", "ty")),
        ),
        check_vma=False,
    )
```

```python
import functools

import jax
import jax.numpy as jnp
from jax import lax
from jax.experimental import pallas as pl
from jax.experimental.pallas import tpu as pltpu
from jax.sharding import PartitionSpec as P

F32 = jnp.float32
BF16 = jnp.bfloat16
MESH = pl.DeviceIdType.MESH

NZ = 48
SZ = 16
CAP = 1024
SWEEPS = 8
SSWEEPS = 6
RELAX = 0.3
SIXTH = 1.0 / 6.0
CHUNK = 512
POINTS = 4352
PCHUNK = 256
ZB = 48
FB = 16
EARLY = 6


def one_hot(key, depth):
    n = key.shape[1]
    rows = lax.broadcasted_iota(jnp.int32, (256, n), 0).astype(BF16)
    parts = []
    for b in range(depth // 256):
        low = jnp.where((key >> 8) == b, key & 255, -1) if depth > 256 else key
        low = jnp.broadcast_to(low.astype(F32).astype(BF16), (256, n))
        parts.append(jnp.where(rows == low, jnp.ones((), BF16), jnp.zeros((), BF16)))
    return jnp.concatenate(parts, axis=0) if len(parts) > 1 else parts[0]


def pieces(v):
    hi = v.astype(BF16)
    return hi, (v - hi.astype(F32)).astype(BF16)


def kernel(
    row,
    rows_tx,
    far_vel,
    far_pre,
    far_drag,
    far_forc,
    far_svel,
    far_spre,
    far_sdrag,
    far_sforc,
    owners,
    counts,
    far_cells,
    far_slots,
    far_weights,
    far_out,
    vel,
    pre,
    drag,
    forc,
    svel,
    spre,
    sdrag,
    sforc,
    cells,
    slots,
    weights,
    flat,
    nvel,
    npre,
    nsvel,
    nspre,
    sidx,
    ridx,
    table,
    rep,
    got,
    table2,
    planes,
    xs,
    xr,
    ys,
    yr,
    pred,
    pxs,
    pxr,
    pys,
    pyr,
    src,
    hs,
    hr,
    hd,
    hm,
    corr,
    step,
    slope,
    sps,
    spr,
    sh,
    wes,
    wer,
    wem,
    rows,
    rim,
    load_sem,
    out_sem,
    idx_send,
    idx_recv,
    rep_send,
    rep_recv,
    halo_send,
    halo_recv,
):
    tx = lax.axis_index("tx")
    ty = lax.axis_index("ty")
    me = tx * row + ty
    total = row * rows_tx

    def device(a, b):
        return {"tx": a, "ty": b}

    def place(d):
        return device(d // row, lax.rem(d, row))

    x_before = device(lax.rem(tx + rows_tx - 1, rows_tx), ty)
    x_after = device(lax.rem(tx + 1, rows_tx), ty)
    y_before = device(tx, lax.rem(ty + row - 1, row))
    y_after = device(tx, lax.rem(ty + 1, row))
    d_before = place(lax.rem(me + total - 1, total))
    d_after = place(lax.rem(me + 1, total))

    loads = {}
    for n, (name, far, near) in enumerate(
        (
            ("cells", far_cells, cells),
            ("vel", far_vel, vel),
            ("pre", far_pre, pre),
            ("svel", far_svel, svel),
            ("spre", far_spre, spre),
            ("sdrag", far_sdrag, sdrag),
            ("sforc", far_sforc, sforc),
            ("drag", far_drag, drag),
            ("forc", far_forc, forc),
            ("slots", far_slots, slots),
            ("weights", far_weights, weights),
        )
    ):
        loads[name] = pltpu.make_async_copy(far, near, load_sem.at[n])
        loads[name].start()

    def loaded(*names):
        for name in names:
            loads[name].wait()

    diagonal = [
        device(there["tx"], side["ty"])
        for there in (x_before, x_after)
        for side in (y_before, y_after)
    ]

    barrier = pltpu.get_barrier_semaphore()
    for t in range(1, row):
        pl.semaphore_signal(
            barrier, inc=1, device_id=device(tx, lax.rem(ty + t, row)), device_id_type=MESH
        )
    for there in (x_before, x_after, d_before, d_after, *diagonal):
        pl.semaphore_signal(barrier, inc=1, device_id=there, device_id_type=MESH)

    lane = lax.broadcasted_iota(jnp.int32, (8, 128), 1)
    sub = lax.broadcasted_iota(jnp.int32, (8, 128), 0)
    zero = jnp.zeros((8, 128), F32)
    left = ((lane >> 3) & 1) == 0

    def up(v):
        return pltpu.roll(v, 1, v.ndim - 1)

    def down(v):
        return pltpu.roll(v, 127, v.ndim - 1)

    def sub_up(v):
        return pltpu.roll(v, 1, v.ndim - 2)

    def sub_down(v):
        return pltpu.roll(v, 7, v.ndim - 2)

    def copy(src_ref, dst_ref, number, there):
        return pltpu.make_async_remote_copy(
            src_ref=src_ref,
            dst_ref=dst_ref,
            send_sem=halo_send.at[number],
            recv_sem=halo_recv.at[number],
            device_id=there,
            device_id_type=MESH,
        )

    field = [vel.at[0], vel.at[1], vel.at[2], pre]

    loaded("cells")
    for p in range(row):
        sidx[p] = cells[p : p + 1, :]

    loaded("vel", "pre")
    for f in range(4):
        xs[0, f] = field[f][:, 0, :]
        xs[1, f] = field[f][:, 7, :]

    def pack_fields(zz, acc):
        acc = list(acc)
        for f in range(4):
            j = f * 16 + zz
            here = (lane >> 1) == j
            for g in range(3):
                acc[g] = jnp.where(
                    here, pltpu.roll(field[f][g * 16 + zz], 2 * j + 1, 1), acc[g]
                )
        return tuple(acc)

    acc = lax.fori_loop(0, 16, pack_fields, (zero,) * 3)
    for g in range(3):
        ys[g] = acc[g]

    sfield = [svel.at[0], svel.at[1], svel.at[2], spre, sdrag, sforc.at[0], sforc.at[1]]

    loaded("svel", "spre", "sdrag", "sforc")

    def pack_site(j, acc):
        acc = list(acc)
        here = (lane >> 4) == j
        for f in range(7):
            for g in range(2):
                acc[2 * f + g] = jnp.where(
                    here, pltpu.roll(sfield[f][g * 8 + j], 16 * j + 8, 1), acc[2 * f + g]
                )
        return tuple(acc)

    acc = lax.fori_loop(0, 8, pack_site, (zero,) * 14)
    for g in range(14):
        sps[g] = acc[g]

    pl.semaphore_wait(barrier, row - 1 + 8)

    def index_copy(to, slot):
        return pltpu.make_async_remote_copy(
            src_ref=sidx.at[to],
            dst_ref=ridx.at[ty],
            send_sem=idx_send.at[to],
            recv_sem=idx_recv.at[slot],
            device_id=device(tx, to),
            device_id_type=MESH,
        )

    for t in range(1, row):
        index_copy(lax.rem(ty + t, row), ty).start()

    fields_x = [copy(xs.at[0], xr.at[1], 0, x_before), copy(xs.at[1], xr.at[0], 1, x_after)]
    fields_y = [copy(ys, yr.at[1], 2, y_before), copy(ys, yr.at[0], 3, y_after)]
    site_y = [copy(sps, spr.at[1], 4, d_before), copy(sps, spr.at[0], 5, d_after)]
    pred_x = [copy(pxs.at[0], pxr.at[1], 6, x_before), copy(pxs.at[1], pxr.at[0], 7, x_after)]
    pred_y = [copy(pys, pyr.at[1], 8, y_before), copy(pys, pyr.at[0], 9, y_after)]
    src_y = [copy(hs, hr.at[1], 10, y_before), copy(hs, hr.at[0], 11, y_after)]
    src_x = [
        copy(src.at[:, 8:16, 0:128], src.at[:, 16:24, 0:128], 12, x_before),
        copy(src.at[:, 8:16, 0:128], src.at[:, 0:8, 0:128], 13, x_after),
    ]
    corner_x = [
        copy(hs, hd.at[1 - n // 2, 1 - n % 2], 14 + n, diagonal[n]) for n in range(4)
    ]
    plane_y = [copy(wes, wer.at[1], 18, d_before), copy(wes, wer.at[0], 19, d_after)]

    def start(pair):
        for c in pair:
            c.start()

    def arrive(pair):
        for c in pair:
            c.wait_recv()

    start(fields_x)
    start(fields_y)
    start(site_y)

    for f in range(4):
        for u in range(NZ // 16):
            for k in range(8):
                z = 16 * u + k
                hi, lo = pieces(jnp.concatenate([field[f][z], field[f][z + 8]], axis=0))
                r = f * NZ + 16 * u
                table[r : r + 16, k * 128 : (k + 1) * 128] = hi
                table[4 * NZ + r : 4 * NZ + r + 16, k * 128 : (k + 1) * 128] = lo

    def lookup(q):
        for c in range(CAP // CHUNK):
            v = ridx[q, :, c * CHUNK : (c + 1) * CHUNK]
            key = (v & 127) | (((v >> 10) & 7) << 7)
            m = ((v >> 13) << 3) | ((v >> 7) & 7)
            found = jnp.dot(table[...], one_hot(key, 1024), preferred_element_type=F32)
            layer = lax.broadcasted_iota(jnp.int32, (NZ, CHUNK), 0) == m
            for f in range(4):
                s = found[f * NZ : (f + 1) * NZ] + found[(4 + f) * NZ : (5 + f) * NZ]
                s = jnp.sum(jnp.where(layer, s, 0.0), axis=0, keepdims=True)
                for k in range(CHUNK // 128):
                    r = c * (CHUNK // 128) + k
                    rep[q, f, r : r + 1, :] = s[:, k * 128 : (k + 1) * 128]

    def reply_copy(to, slot):
        return pltpu.make_async_remote_copy(
            src_ref=rep.at[to],
            dst_ref=got.at[ty],
            send_sem=rep_send.at[to],
            recv_sem=rep_recv.at[slot],
            device_id=device(tx, to),
            device_id_type=MESH,
        )

    def serve(t, _):
        q = lax.rem(ty + row - t, row)
        index_copy(q, q).wait_recv()
        lookup(q)
        reply_copy(q, ty).start()
        return 0

    ridx[ty] = sidx[ty]
    lookup(ty)
    got[ty] = rep[ty]

    def open_site():
        for g in range(14):
            spr[0, g] = jnp.where(left, spr[0, g], spr[1, g])
        for n in range(7 * SZ):
            sh[n // SZ, n % SZ] = pltpu.roll(spr[0, n // 8], (120 - 16 * (n % 8)) % 128, 1)

    def open_slots():
        loaded("slots", "weights")
        flat[...] = weights[...].reshape(1, POINTS)
        for n in range(2 * SZ):
            at = pl.ds(n * 128, 128)
            rows[0, n : n + 1, :] = slots[0:1, at]
            rows[1, n : n + 1, :] = slots[1:2, at]
            rows[2, n : n + 1, :] = flat[:, at]
        for r in range(3):
            v = jnp.zeros((8, 128), jnp.int32)
            for g in range(4):
                v = jnp.where(
                    (lane >> 4) == g, pltpu.roll(rows[r, 8 * g : 8 * g + 8, :], 16 * g + 8, 1), v
                )
            rim[r] = v

    has_x = [jnp.where(tx > 0, 1.0, 0.0), jnp.where(tx < rows_tx - 1, 1.0, 0.0)]
    has_y = [jnp.where(ty > 0, 1.0, 0.0), jnp.where(ty < row - 1, 1.0, 0.0)]
    edge_y = jnp.where(lane < 64, has_y[0], has_y[1])

    lax.fori_loop(1, 4, serve, 0)

    loaded("drag", "forc")
    arrive(fields_x)
    arrive(fields_y)
    for g in range(3):
        first = (lane & 1) == 0
        yr[0, g] = jnp.where(first, down(yr[1, g]), up(yr[0, g]))

    def below(ref, z):
        v = ref[jnp.maximum(z - 1, 0)]
        return v * jnp.where(z > 0, 1.0, 0.0)

    def above(ref, z):
        v = ref[jnp.minimum(z + 1, NZ - 1)]
        return v * jnp.where(z < NZ - 1, 1.0, 0.0)

    def x_sides(v, low, high):
        low = jnp.broadcast_to(low, (8, 128)) * has_x[0]
        high = jnp.broadcast_to(high, (8, 128)) * has_x[1]
        return jnp.where(sub == 0, low, sub_up(v)), jnp.where(sub == 7, high, sub_down(v))

    def y_sides(v, edge):
        edge = edge * edge_y
        return jnp.where(lane == 0, edge, up(v)), jnp.where(lane == 127, edge, down(v))

    def predict(zz, packed):
        for g in range(3):
            z = g * 16 + zz
            inverse = 1.0 / (6.0 + drag[z])
            sides = []
            for f in range(4):
                v = field[f][z]
                xm, xp = x_sides(v, xr[0, f, pl.ds(z, 1), :], xr[1, f, pl.ds(z, 1), :])
                k = 2 * (f * 16 + zz) + 1
                ym, yp = y_sides(v, pltpu.roll(yr[0, g], 128 - k, 1))
                sides.append((xm, xp, ym, yp, below(field[f], z), above(field[f], z)))
            push = sides[3]
            push = [(push[1] - push[0]) * 0.5, (push[3] - push[2]) * 0.5, (push[5] - push[4]) * 0.5]
            out = []
            for i in range(3):
                s = sides[i]
                n = ((s[0] + s[1]) + (s[2] + s[3])) + (s[4] + s[5])
                if i < 2:
                    n = n + forc[i, z]
                out.append((n - push[i]) * inverse)
                pred[i, z] = out[i]
            packed = jnp.where((lane >> 1) == z, pltpu.roll(out[1], 2 * z + 1, 1), packed)
        return packed

    def serve_predict(i, packed):
        serve(4 + i, 0)
        for zz in range(8):
            packed = predict(i * 8 + zz, packed)
        return packed

    pys[...] = lax.fori_loop(0, 2, serve_predict, zero)
    pxs[0] = pred[0, :, 0, :]
    pxs[1] = pred[0, :, 7, :]
    start(pred_x)
    start(pred_y)

    lax.fori_loop(6, 10, serve, 0)

    arrive(pred_x)
    arrive(pred_y)
    first = (lane & 1) == 0
    edges_v = jnp.where(first, down(pyr[1]), up(pyr[0]))

    def source(j, packed):
        packed = list(packed)
        for g in range(6):
            z = g * 8 + j
            xm, xp = x_sides(pred[0, z], pxr[0, pl.ds(z, 1), :], pxr[1, pl.ds(z, 1), :])
            ym, yp = y_sides(pred[1, z], pltpu.roll(edges_v, 127 - 2 * z, 1))
            div = (xp - xm) + (yp - ym) + (above(pred.at[2], z) - below(pred.at[2], z))
            s = div * 0.5 * (6.0 + drag[z])
            src[z, 8:16, 0:128] = s
            packed[g] = jnp.where((lane >> 4) == j, pltpu.roll(s, 16 * j + 8, 1), packed[g])
        return tuple(packed)

    serve(10, 0)
    acc = (zero,) * 6
    for j in range(8):
        acc = source(j, acc)
    for g in range(6):
        hs[g] = acc[g]
    start(src_y)
    start(corner_x)
    start(src_x)

    serve(11, 0)
    open_slots()
    serve(12, 0)
    arrive(site_y)
    serve(13, 0)
    open_site()
    serve(14, 0)

    arrive(src_y)
    arrive(corner_x)
    for g in range(6):
        hm[0, g] = jnp.where(left, hd[0, 0, g], hd[0, 1, g])
        hm[1, g] = jnp.where(left, hr[0, g], hr[1, g])
        hm[2, g] = jnp.where(left, hd[1, 0, g], hd[1, 1, g])

    arrive(src_x)
    inside = []
    for b in range(3):
        m = (has_x[0], 1.0, has_x[1])[b] * SIXTH
        inside.append(
            jnp.concatenate([jnp.full((8, 128), m, F32), edge_flip(lane, has_y) * m], axis=1)
        )
    inside = jnp.concatenate(inside, axis=0)[None]

    for n in range(2):
        corr[n, 0] = jnp.zeros((40, 256), F32)
        corr[n, NZ + 1] = jnp.zeros((40, 256), F32)
        corr[n, 1 : NZ + 1, 0:8, :] = jnp.zeros((NZ, 8, 256), F32)
        corr[n, 1 : NZ + 1, 32:40, :] = jnp.zeros((NZ, 8, 256), F32)

    def widen(j, _):
        for b in range(3):
            for g in range(6):
                z = g * 8 + j
                s = pltpu.roll(hm[b, g], 120 - 16 * j, 1)
                m = inside[0, 8 * b : 8 * b + 8]
                src[z, 8 * b : 8 * b + 8, 128:256] = s
                corr[1, z + 1, 8 * b + 8 : 8 * b + 16, 0:128] = (
                    -src[z, 8 * b : 8 * b + 8, 0:128] * m[:, :128]
                )
                corr[1, z + 1, 8 * b + 8 : 8 * b + 16, 128:256] = -s * m[:, 128:]
        return 0

    serve(15, 0)
    for j in range(8):
        widen(j, 0)

    at = lax.broadcasted_iota(jnp.int32, (256, 256), 0)
    to = lax.broadcasted_iota(jnp.int32, (256, 256), 1)
    after = jnp.where(((at - to) & 255) == 1, 1.0, 0.0)
    before = jnp.where(((to - at) & 255) == 1, 1.0, 0.0)
    both = (after + before).astype(BF16)
    step[0:256, :] = both
    step[256:512, :] = both
    slope[0:256, :] = (after - before)[:, :128].astype(BF16)
    slope[256:512, :] = (after - before)[:, :128].astype(BF16)

    def apply(v, matrix):
        layers, rows, lanes = v.shape
        hi, lo = pieces(v.reshape(layers * rows, lanes))
        out = jnp.dot(
            jnp.concatenate([hi, lo], axis=1), matrix[...], preferred_element_type=F32
        )
        return out.reshape(layers, rows, out.shape[1])

    def sweep(k):
        now, later = k % 2, (k + 1) % 2
        first, rows = (0, 24) if SWEEPS - k > 4 else (4, 16)
        lo, hi = first + 8, first + 8 + rows
        for i in range(NZ // ZB):
            z = i * ZB
            n = apply(corr[now, z + 1 : z + 1 + ZB, lo:hi, :], step)
            n = n + (
                corr[now, z + 1 : z + 1 + ZB, lo - 1 : hi - 1, :]
                + corr[now, z + 1 : z + 1 + ZB, lo + 1 : hi + 1, :]
            )
            n = n + (corr[now, z : z + ZB, lo:hi, :] + corr[now, z + 2 : z + 2 + ZB, lo:hi, :])
            n = n - src[z : z + ZB, first : first + rows, :]
            corr[later, z + 1 : z + 1 + ZB, lo:hi, :] = n * inside[:, first : first + rows]

    for k in range(1, EARLY):
        sweep(k)

    for t in range(1, row):
        q = lax.rem(ty + row - t, row)
        reply_copy(q, q).wait_recv()
    for f in range(4):
        for b in range(2):
            for u in range(row // 4):
                v = jnp.concatenate([got[4 * u + b, f], got[4 * u + 2 + b, f]], axis=0)
                hi, lo = pieces(v)
                r = f * 4 * row + u * 16
                table2[r : r + 16, b * 128 : (b + 1) * 128] = hi
                table2[16 * row + r : 16 * row + r + 16, b * 128 : (b + 1) * 128] = lo

    def point(j, w):
        n = w.shape[1]
        key = (j & 127) | (((j >> 10) & 1) << 7)
        m = ((j >> 11) << 3) | ((j >> 7) & 7)
        found = jnp.dot(table2[...], one_hot(key, 256), preferred_element_type=F32)
        here = lax.broadcasted_iota(jnp.int32, (4 * row, 2 * n), 0) == m
        w = (2.0 * w.astype(F32) + 1.0) * 0.125
        out = []
        for f in range(4):
            r = f * 4 * row
            s = found[r : r + 4 * row] + found[16 * row + r : 16 * row + r + 4 * row]
            s = jnp.sum(jnp.where(here, s, 0.0), axis=0, keepdims=True)
            out.append(w * s[:, :n] + (1.0 - w) * s[:, n:])
        return out

    for c in range(4):
        r = [rim[k, 2 * c + i : 2 * c + i + 1, :] for k in range(3) for i in range(2)]
        out = point(jnp.concatenate(r[:4], axis=1), jnp.concatenate(r[4:], axis=1))
        for f in range(4):
            wes[f, 2 * c : 2 * c + 1, :] = out[f][:, :128]
            wes[f, 2 * c + 1 : 2 * c + 2, :] = out[f][:, 128:]
    start(plane_y)

    for c in range(POINTS // PCHUNK):
        at = pl.ds(c * PCHUNK, PCHUNK)
        out = point(jnp.concatenate([slots[0:1, at], slots[1:2, at]], axis=1), flat[:, at])
        for f in range(4):
            planes[f, 2 * c : 2 * c + 1, :] = out[f][:, :128]
            planes[f, 2 * c + 1 : 2 * c + 2, :] = out[f][:, 128:]
    sweep(EARLY)

    for k in range(EARLY + 1, SWEEPS):
        sweep(k)
    last = SWEEPS % 2

    def finish(i, _):
        z = i * FB
        c = corr[last, pl.ds(z + 1, FB), 16:24, :]
        gy = apply(c, slope)
        gx = corr[last, pl.ds(z + 1, FB), 17:25, :128] - corr[last, pl.ds(z + 1, FB), 15:23, :128]
        gz = corr[last, pl.ds(z + 2, FB), 16:24, :128] - corr[last, pl.ds(z, FB), 16:24, :128]
        half = 0.5 / (6.0 + drag[pl.ds(z, FB)])
        nvel[0, pl.ds(z, FB)] = pred[0, pl.ds(z, FB)] - gx * half
        nvel[1, pl.ds(z, FB)] = pred[1, pl.ds(z, FB)] - gy * half
        nvel[2, pl.ds(z, FB)] = pred[2, pl.ds(z, FB)] - gz * half
        npre[pl.ds(z, FB)] = pre[pl.ds(z, FB)] + RELAX * c[:, :, :128]
        return 0

    lax.fori_loop(0, NZ // FB, finish, 0)

    stores = []
    for n in range(8):
        near = (nvel.at[0], nvel.at[1], nvel.at[2], npre, nsvel.at[0], nsvel.at[1], nsvel.at[2], nspre)[n]
        first = n * NZ if n < 4 else 4 * NZ + (n - 4) * SZ
        size = NZ if n < 4 else SZ
        stores.append(pltpu.make_async_copy(near, far_out.at[first : first + size], out_sem.at[n]))
    for n in range(4):
        stores[n].start()

    own = owners[me]
    begins = (me == 0) | (owners[jnp.maximum(me - 1, 0)] != own)
    ends = (me == total - 1) | (owners[jnp.minimum(me + 1, total - 1)] != own)
    begins = jnp.full((8, 128), begins.astype(F32), F32)
    ends = jnp.full((8, 128), ends.astype(F32), F32)
    allowed = jnp.full((8, 128), counts[own], jnp.int32)
    other = jnp.where(lane < 64, ends, begins) > 0.5

    def ends_of(f):
        s = jnp.where((lane & 7) == sub, jnp.broadcast_to(planes[f, 32:33, :], (8, 128)), 0.0)
        n = jnp.where((lane & 7) == sub, jnp.broadcast_to(planes[f, 33:34, :], (8, 128)), 0.0)
        for k in (1, 2, 4):
            s = s + pltpu.roll(s, k, 1)
            n = n + pltpu.roll(n, 128 - k, 1)
        both = jnp.where((lane & 7) == 7, s, pltpu.roll(n, 8, 1))
        return [pltpu.roll(both, (120 - 8 * z) % 128, 1) for z in range(SZ)]

    outer = [jnp.stack(ends_of(f)) for f in range(4)]
    edge_lane = (lane == 0) | (lane == 127)

    def with_ends(v, f):
        return jnp.where((edge_lane & other)[None], outer[f], v)

    arrive(plane_y)
    for f in range(4):
        v = jnp.where(left, wer[0, f], wer[1, f])
        for g in range(4):
            wem[f, 8 * g : 8 * g + 8, :] = pltpu.roll(v, 120 - 16 * g, 1)

    west = [[planes[f, 0:SZ, :], wem[f, 0:SZ, :]] for f in range(4)]
    east = [[planes[f, SZ : 2 * SZ, :], wem[f, SZ : 2 * SZ, :]] for f in range(4)]

    def layer_sides(v):
        blank = jnp.zeros((1, 8, 128), F32)
        return jnp.concatenate([blank, v[:-1]], axis=0), jnp.concatenate([v[1:], blank], axis=0)

    def site_x(v, h, f):
        shape = (SZ, 8, 128)
        if f is None:
            low = high = jnp.zeros(shape, F32)
        else:
            low = jnp.broadcast_to(west[f][h][:, None, :], shape)
            high = jnp.broadcast_to(east[f][h][:, None, :], shape)
        return jnp.where(sub[None] == 0, low, sub_up(v)), jnp.where(sub[None] == 7, high, sub_down(v))

    def site_y_sides(pair):
        u = [up(v) for v in pair]
        d = [down(v) for v in pair]
        return [
            (
                jnp.where(lane[None] == 0, u[1 - h], u[h]),
                jnp.where(lane[None] == 127, d[1 - h], d[h]),
            )
            for h in range(2)
        ]

    fields = [[sfield[f][...], with_ends(sh[f], f)] for f in range(4)]
    diag = [6.0 + sdrag[...], 6.0 + sh[4]]
    inverse = [1.0 / v for v in diag]
    force = [[sforc[i], sh[5 + i]] for i in range(2)]
    xside = [[site_x(fields[f][h], h, f) for h in range(2)] for f in range(4)]
    yside = [site_y_sides(fields[f]) for f in range(4)]
    moved = [[None, None] for _ in range(3)]
    for h in range(2):
        below_p, above_p = layer_sides(fields[3][h])
        push = [
            (xside[3][h][1] - xside[3][h][0]) * 0.5,
            (yside[3][h][1] - yside[3][h][0]) * 0.5,
            (above_p - below_p) * 0.5,
        ]
        for i in range(3):
            lo, hi = layer_sides(fields[i][h])
            n = (xside[i][h][0] + xside[i][h][1]) + (yside[i][h][0] + yside[i][h][1]) + (lo + hi)
            if i < 2:
                n = n + force[i][h]
            v = (n - push[i]) * inverse[h]
            moved[i][h] = with_ends(v, i) if h == 1 else v

    ys_v = site_y_sides(moved[1])
    term = []
    for h in range(2):
        xm, xp = site_x(moved[0][h], h, 0)
        lo, hi = layer_sides(moved[2][h])
        term.append(((xp - xm) + (ys_v[h][1] - ys_v[h][0]) + (hi - lo)) * 0.5 * diag[h])

    keep = [
        jnp.full((1, 8, 128), SIXTH, F32),
        jnp.where(other, 0.0, SIXTH)[None],
    ]
    e = [-term[h] * keep[h] for h in range(2)]
    for k in range(1, SSWEEPS):
        sides = site_y_sides(e)
        fresh = []
        for h in range(2):
            xm, xp = site_x(e[h], h, None)
            lo, hi = layer_sides(e[h])
            n = (xm + xp) + (sides[h][0] + sides[h][1]) + (lo + hi)
            fresh.append(jnp.where((allowed > k)[None], (n - term[h]) * keep[h], e[h]))
        e = fresh
    xm, xp = site_x(e[0], 0, None)
    ym, yp = site_y_sides(e)[0]
    lo, hi = layer_sides(e[0])
    half = 0.5 * inverse[0]
    nsvel[0] = moved[0][0] - (xp - xm) * half
    nsvel[1] = moved[1][0] - (yp - ym) * half
    nsvel[2] = moved[2][0] - (hi - lo) * half
    nspre[...] = spre[...] + RELAX * e[0]

    for n in range(4, 8):
        stores[n].start()

    for pair in (fields_x, fields_y, site_y, pred_x, pred_y, src_y, src_x, corner_x, plane_y):
        for c in pair:
            c.wait_send()
    for t in range(1, row):
        q = lax.rem(ty + t, row)
        index_copy(q, q).wait_send()
        reply_copy(q, q).wait_send()
    for c in stores:
        c.wait()


def spread(far, nvel, npre, nsvel, nspre, held, sem):
    places = (nvel.at[0], nvel.at[1], nvel.at[2], npre)
    places += (nsvel.at[0], nsvel.at[1], nsvel.at[2], nspre)
    first, moves = 0, []
    for n, place in enumerate(places):
        part = pl.ds(first, place.shape[0])
        moves.append(
            (
                pltpu.make_async_copy(far.at[part], held.at[part], sem.at[0, n]),
                pltpu.make_async_copy(held.at[part], place, sem.at[1, n]),
            )
        )
        first += place.shape[0]
    for come, _ in moves:
        come.start()
    for come, go in moves:
        come.wait()
        go.start()
    for _, go in moves:
        go.wait()


def edge_flip(lane, has_y):
    return jnp.where(lane < 64, has_y[1], has_y[0])


def shards(
    velocity,
    pressure,
    drag_rate,
    forcing,
    site_velocity,
    site_pressure,
    site_drag,
    site_forcing,
    owners,
    sweep_counts,
    parent_cells,
    point_slots,
    point_weights,
):
    row = lax.axis_size("ty")
    rows_tx = lax.axis_size("tx")
    sm = pl.BlockSpec(memory_space=pltpu.SMEM)
    hbm = pl.BlockSpec(memory_space=pl.ANY)

    def v(*shape):
        return pltpu.VMEM(shape, F32)

    both = pl.pallas_call(
        functools.partial(kernel, row, rows_tx),
        out_shape=jax.ShapeDtypeStruct((4 * (NZ + SZ), 8, 128), F32),
        in_specs=[hbm] * 8 + [sm] * 2 + [hbm] * 3,
        out_specs=hbm,
        scratch_shapes=[
            v(3, NZ, 8, 128),
            v(NZ, 8, 128),
            v(NZ, 8, 128),
            v(2, NZ, 8, 128),
            v(3, SZ, 8, 128),
            v(SZ, 8, 128),
            v(SZ, 8, 128),
            v(2, SZ, 8, 128),
            pltpu.VMEM((row, CAP), jnp.int32),
            pltpu.VMEM((2, POINTS), jnp.int32),
            pltpu.VMEM((POINTS,), jnp.int32),
            pltpu.VMEM((1, POINTS), jnp.int32),
            v(3, NZ, 8, 128),
            v(NZ, 8, 128),
            v(3, SZ, 8, 128),
            v(SZ, 8, 128),
            pltpu.VMEM((row, 1, CAP), jnp.int32),
            pltpu.VMEM((row, 1, CAP), jnp.int32),
            pltpu.VMEM((8 * NZ, 1024), BF16),
            v(row, 4, 8, 128),
            v(row, 4, 8, 128),
            pltpu.VMEM((32 * row, 256), BF16),
            v(4, 40, 128),
            v(2, 4, NZ, 128),
            v(2, 4, NZ, 128),
            v(3, 8, 128),
            v(2, 3, 8, 128),
            v(3, NZ, 8, 128),
            v(2, NZ, 128),
            v(2, NZ, 128),
            v(8, 128),
            v(2, 8, 128),
            v(NZ, 24, 256),
            v(6, 8, 128),
            v(2, 6, 8, 128),
            v(2, 2, 6, 8, 128),
            v(3, 6, 8, 128),
            v(2, NZ + 2, 40, 256),
            pltpu.VMEM((512, 256), BF16),
            pltpu.VMEM((512, 128), BF16),
            v(14, 8, 128),
            v(2, 14, 8, 128),
            v(7, SZ, 8, 128),
            v(4, 8, 128),
            v(2, 4, 8, 128),
            v(4, 2 * SZ, 128),
            pltpu.VMEM((3, 2 * SZ, 128), jnp.int32),
            pltpu.VMEM((3, 8, 128), jnp.int32),
            pltpu.SemaphoreType.DMA((11,)),
            pltpu.SemaphoreType.DMA((8,)),
            pltpu.SemaphoreType.DMA((row,)),
            pltpu.SemaphoreType.DMA((row,)),
            pltpu.SemaphoreType.DMA((row,)),
            pltpu.SemaphoreType.DMA((row,)),
            pltpu.SemaphoreType.DMA((20,)),
            pltpu.SemaphoreType.DMA((20,)),
        ],
        compiler_params=pltpu.CompilerParams(
            collective_id=0, has_side_effects=True, vmem_limit_bytes=60 * 2**20
        ),
        name="wind_step",
    )(
        velocity,
        pressure,
        drag_rate,
        forcing,
        site_velocity,
        site_pressure,
        site_drag,
        site_forcing,
        owners,
        sweep_counts,
        parent_cells,
        point_slots,
        point_weights,
    )
    return pl.pallas_call(
        spread,
        out_shape=[
            jax.ShapeDtypeStruct(a.shape, F32)
            for a in (velocity, pressure, site_velocity, site_pressure)
        ],
        in_specs=[hbm],
        out_specs=[hbm] * 4,
        scratch_shapes=[v(4 * (NZ + SZ), 8, 128), pltpu.SemaphoreType.DMA((2, 8))],
        name="spread",
    )(both)


def solution(mesh):
    placed = (
        P(None, None, "tx", "ty"),
        P(None, "tx", "ty"),
        P(None, "tx", "ty"),
        P(None, None, "tx", "ty"),
        P(None, None, None, ("tx", "ty")),
        P(None, None, ("tx", "ty")),
        P(None, None, ("tx", "ty")),
        P(None, None, None, ("tx", "ty")),
        P(),
        P(),
        P(("tx", "ty"), None),
        P(None, ("tx", "ty")),
        P(("tx", "ty")),
    )
    return jax.shard_map(
        shards,
        mesh=mesh,
        in_specs=placed,
        out_specs=(
            P(None, None, "tx", "ty"),
            P(None, "tx", "ty"),
            P(None, None, None, ("tx", "ty")),
            P(None, None, ("tx", "ty")),
        ),
        check_vma=False,
    )
```
